512 devices in a mesh: trc: 32 (over z_hi, y, x), lev: 16 (over z_lo, core).
Axes of the slice: x: 4, y: 4, z: 16 (z_hi: 2, z_lo: 8; z = z_hi * 8 + z_lo), core: 2. Of those that a mesh axis runs over, the one named last changes fastest.
Arguments:
- tracers: float32 [64, 256, 4, 32, 128], P('lev', 'trc'), may hold values from -6 to 6
- air_mass: float32 [64, 32, 128], P('lev'), may hold values from 2 to 3
- mass_flux: float32 [3, 64, 32, 128], P(None, 'lev', 'trc'), may hold values from -0.3 to 0.3
- chem_inverse: bfloat16 [4, 256, 256], replicated, as said below
- chem_source: float32 [4, 256], replicated, may hold values from -3 to 3
- reaction_set: int32 [64, 32, 128], P('lev', 'trc'), may hold values from 0 to 3
- chem_steps: int32 [64, 32, 128], P('lev', 'trc'), may hold values from 1 to 6
Outputs:
- tracers_out: float32 [64, 256, 4, 32, 128], P('lev', 'trc')
The draws below stay inside these ranges and needn't reach their ends.
Inputs may be any that keep to these rules, and one draw needn't show every extreme that they name: `chem_inverse`: the diagonal lies in 0.3 to 0.8, every other entry is small.
All inputs are finite; a program needn't handle non-finite values.
Results may differ from the reference program's by a relative error of at most 0.0016.
Values sent between devices are 32-bit elements; how exact they have to be, the bound alone decides.
A program may use at most 64 MiB of HBM per device.

```python
import math
import jax
import jax.numpy as jnp
from jax import lax

TRACERS = 256
LAT = 32
LON = 128
RSETS = 4
NSTEP = 6
LEVELS = 64


def draw_chem_inverse(key, part):
    key = jax.random.fold_in(key, 11)
    key_diag, key_off = jax.random.split(key)
    diagonal = jax.random.uniform(key_diag, (RSETS, TRACERS), jnp.float32, 0.3, 0.8)
    diagonal = diagonal.at[:, 0].set(0.8)
    spread = 0.3 / math.sqrt(TRACERS)
    off_part = jax.random.truncated_normal(key_off, -4.0, 4.0, (RSETS, TRACERS, TRACERS), jnp.float32) * spread
    identity = jnp.eye(TRACERS, dtype=jnp.float32)
    whole = off_part * (1.0 - identity) + identity * diagonal[:, :, None]
    return whole.astype(jnp.bfloat16)


def draw_chem_steps(key, part):
    key = jax.random.fold_in(key, 12)
    values = jax.random.randint(key, (LEVELS * LAT * LON,), 1, NSTEP + 1, jnp.int32)
    values = values.at[0].set(NSTEP).at[1].set(1)
    return values.reshape(LEVELS, LAT, LON)


def with_ends(values, rng, least, top_value):
    dims = values.shape
    spot = [jax.random.randint(jax.random.fold_in(rng, axis), (), 0, dims[axis]) for axis in range(len(dims))]
    values = values.at[tuple(spot)].set(least)
    longest = dims.index(max(dims))
    spot[longest] = (spot[longest] + 1) % dims[longest]
    return values.at[tuple(spot)].set(top_value)


def block_levels(key, dims, cuts, smallest, top_value):
    def one(position, shards_of):
        steps = jax.random.uniform(jax.random.fold_in(jax.random.fold_in(key, 6), position), (shards_of,), jnp.float32, smallest / len(cuts), top_value / len(cuts))
        return jnp.repeat(jnp.exp(steps), dims[position] // shards_of).reshape((-1,) + (1,) * (len(dims) - position - 1))

    loudness = one(*cuts[0])
    for cut in cuts[1:]:
        loudness = loudness * one(*cut)
    return loudness


def gaussian(rng, extent, scale, most, pieces=(), held_as=jnp.bfloat16):
    level = block_levels(rng, extent, pieces, -0.22, 0.18) if pieces else 1.0
    values = jax.random.normal(rng, extent, jnp.float32) * scale * level
    return jnp.minimum(jnp.maximum(values, -most), most).astype(held_as)


def setup_inputs(seed: int = 0) -> dict:
    seeds = jax.random.split(jax.random.key(seed), 8)
    tracers = gaussian(seeds[0], (LEVELS, TRACERS, 4, LAT, LON), 1.0, 6.0, ((0, 16), (1, 32)), jnp.float32)
    air_mass = jnp.clip(2.0 + 1.0 * jax.random.uniform(seeds[1], (LEVELS, LAT, LON), jnp.float32) ** block_levels(seeds[1], (LEVELS, LAT, LON), ((0, 16),), -0.2, 0.2), 2.0, 3.0)
    mass_flux = jnp.clip(jax.random.uniform(seeds[2], (3, LEVELS, LAT, LON), jnp.float32, -0.3, 0.3) * block_levels(seeds[2], (3, LEVELS, LAT, LON), ((1, 16), (2, 32)), -0.4, 0.0), -0.3, 0.3)
    chem_inverse = draw_chem_inverse(jax.random.fold_in(seeds[7], 71), 0)
    chem_source = gaussian(seeds[4], (RSETS, TRACERS), 0.5, 3.0, (), jnp.float32)
    reaction_set = with_ends(jax.random.randint(seeds[5], (LEVELS, LAT, LON), 0, RSETS), jax.random.fold_in(seeds[5], 1), 0, RSETS - 1).astype(jnp.int32)
    chem_steps = draw_chem_steps(jax.random.fold_in(seeds[7], 71), 0)
    return dict(tracers=tracers, air_mass=air_mass, mass_flux=mass_flux, chem_inverse=chem_inverse, chem_source=chem_source, reaction_set=reaction_set, chem_steps=chem_steps)


def shift_down(values, sweep_axis):
    length = values.shape[sweep_axis]
    filler = jnp.zeros_like(lax.slice_in_dim(values, 0, 1, axis=sweep_axis))
    return jnp.concatenate([filler, lax.slice_in_dim(values, 0, length - 1, axis=sweep_axis)], axis=sweep_axis)


def shift_up(values, sweep_axis):
    length = values.shape[sweep_axis]
    filler = jnp.zeros_like(lax.slice_in_dim(values, 0, 1, axis=sweep_axis))
    return jnp.concatenate([lax.slice_in_dim(values, 1, length, axis=sweep_axis), filler], axis=sweep_axis)


def close_wall(fluxes, sweep_axis):
    places = lax.broadcasted_iota(jnp.int32, fluxes.shape, sweep_axis)
    return jnp.where(places < fluxes.shape[sweep_axis] - 1, fluxes, jnp.float32(0.0))


def piece_right(mixing, moment, across, beyond, airmass, fluxes):
    carried = jnp.maximum(fluxes, 0.0)
    fraction = carried / jnp.maximum(airmass, 0.5)
    return carried, mixing + moment * (1.0 - fraction), fraction * moment, across, beyond


def piece_left(mixing, moment, across, beyond, airmass, fluxes):
    carried = jnp.maximum(-fluxes, 0.0)
    fraction = carried / jnp.maximum(airmass, 0.5)
    return carried, mixing - moment * (1.0 - fraction), fraction * moment, across, beyond


def compose(mixing, moment, across, beyond, airmass, upper_flux, lower_flux, incoming_left, incoming_right):
    frac_right = jnp.maximum(upper_flux, 0.0) / airmass
    frac_left = jnp.maximum(-lower_flux, 0.0) / airmass
    remain = 1.0 - frac_left - frac_right
    centre = 0.5 * (frac_left - frac_right)
    remain_mean = mixing + 2.0 * moment * centre
    remain_slope = remain * moment
    remain_air = airmass * remain
    mass_left, mean_left, slope_left, across_left, beyond_left = incoming_left
    mass_right, mean_right, slope_right, across_right, beyond_right = incoming_right
    new_air = mass_left + remain_air + mass_right
    share_left = mass_left / new_air
    share_kept = remain_air / new_air
    share_right = mass_right / new_air
    centre_left = -0.5 + 0.5 * share_left
    centre_kept = -0.5 + share_left + 0.5 * share_kept
    centre_right = 0.5 - 0.5 * share_right
    new_mixing = share_left * mean_left + share_kept * remain_mean + share_right * mean_right
    first_moment = share_left * (centre_left * mean_left + share_left * slope_left / 6.0)
    first_moment = first_moment + share_kept * (centre_kept * remain_mean + share_kept * remain_slope / 6.0)
    first_moment = first_moment + share_right * (centre_right * mean_right + share_right * slope_right / 6.0)
    new_across = share_left * across_left + share_kept * across + share_right * across_right
    new_beyond = share_left * beyond_left + share_kept * beyond + share_right * beyond_right
    return new_mixing, 6.0 * first_moment, new_across, new_beyond, new_air


def advect_sweep(mixing, moment, across, beyond, airmass, fluxes, sweep_axis):
    lower_flux = shift_down(fluxes, sweep_axis)
    lower_cells = [shift_down(values, sweep_axis) for values in (mixing, moment, across, beyond, airmass)]
    upper_cells = [shift_up(values, sweep_axis) for values in (mixing, moment, across, beyond, airmass)]
    incoming_left = piece_right(*lower_cells, lower_flux)
    incoming_right = piece_left(*upper_cells, fluxes)
    return compose(mixing, moment, across, beyond, airmass, fluxes, lower_flux, incoming_left, incoming_right)


def reference(tracers, air_mass, mass_flux, chem_inverse, chem_source, reaction_set, chem_steps):
    airmass = air_mass[:, None]
    flux_x = close_wall(mass_flux[0][:, None], 3)
    flux_y = close_wall(mass_flux[1][:, None], 2)
    flux_z = close_wall(mass_flux[2][:, None], 0)

    def advect_group(index_group, result):
        start = (index_group * 8).astype(jnp.int32)
        tracer_block = lax.dynamic_slice_in_dim(tracers, start, 8, axis=1)
        mixing = tracer_block[:, :, 0]
        slope_x = tracer_block[:, :, 1]
        slope_y = tracer_block[:, :, 2]
        slope_z = tracer_block[:, :, 3]
        mixing, slope_x, slope_y, slope_z, air_now = advect_sweep(mixing, slope_x, slope_y, slope_z, airmass, flux_x, 3)
        mixing, slope_y, slope_x, slope_z, air_now = advect_sweep(mixing, slope_y, slope_x, slope_z, air_now, flux_y, 2)
        mixing, slope_z, slope_x, slope_y, air_now = advect_sweep(mixing, slope_z, slope_x, slope_y, air_now, flux_z, 0)
        return lax.dynamic_update_slice_in_dim(result, jnp.stack([mixing, slope_x, slope_y, slope_z], 2), start, axis=1)

    result = lax.fori_loop(0, TRACERS // 8, advect_group, jnp.zeros_like(tracers))
    inverse_wide = chem_inverse.astype(jnp.float32)
    zero_index = jnp.zeros((), jnp.int32)

    def chem_level(level, result):
        level = level.astype(jnp.int32)
        plane = lax.dynamic_index_in_dim(result, level, 0, keepdims=False)
        columns = plane[:, 0].reshape(TRACERS, LAT * LON)
        set_ids = lax.dynamic_index_in_dim(reaction_set, level, 0, keepdims=False).reshape(-1)
        counts = lax.dynamic_index_in_dim(chem_steps, level, 0, keepdims=False).reshape(-1)
        select = (set_ids[None, :] == jnp.arange(RSETS, dtype=jnp.int32)[:, None]).astype(jnp.float32)
        for substep in range(NSTEP):
            rounded = lax.optimization_barrier(columns.astype(jnp.bfloat16)).astype(jnp.float32)
            product = jnp.einsum("rts,sc->rtc", inverse_wide, rounded, precision=lax.Precision.HIGHEST)
            product = product + chem_source[:, :, None]
            updated = jnp.sum(select[:, None, :] * product, 0)
            columns = jnp.where(substep < counts[None, :], updated, columns)
        fresh = columns.reshape(1, TRACERS, 1, LAT, LON)
        return lax.dynamic_update_slice(result, fresh, (level, zero_index, zero_index, zero_index, zero_index))

    return lax.fori_loop(0, LEVELS, chem_level, result)
```

```python
import jax
import jax.numpy as jnp
from jax import lax
from jax.experimental import pallas as pl
from jax.experimental.pallas import tpu as pltpu
from jax.sharding import PartitionSpec as P

MESH = pl.DeviceIdType.MESH
F32 = jnp.float32
LEV, TRC, LAT, LON = 4, 8, 32, 128
HALF = 16
NT, SETS, NSTEP = 256, 4, 6
PACK = 24


def lower_of(value, axis):
    return pltpu.roll(value, 1, axis)


def upper_of(value, axis):
    return pltpu.roll(value, value.shape[axis] - 1, axis)


def coefficients(air_below, air, air_above, lower, upper):
    from_below = jnp.maximum(lower, 0.0)
    from_above = jnp.maximum(-upper, 0.0)
    fraction_below = from_below / jnp.maximum(air_below, 0.5)
    fraction_above = from_above / jnp.maximum(air_above, 0.5)
    inverse = 1.0 / air
    out_up = jnp.maximum(upper, 0.0) * inverse
    out_down = jnp.maximum(-lower, 0.0) * inverse
    remain = 1.0 - out_down - out_up
    kept = air * remain
    new_air = from_below + kept + from_above
    inverse = 1.0 / new_air
    share_l, share_0, share_r = from_below * inverse, kept * inverse, from_above * inverse
    six_l, six_0, six_r = 6.0 * share_l, 6.0 * share_0, 6.0 * share_r
    return (
        new_air,
        (1.0 - fraction_below, out_down - out_up, fraction_above - 1.0, share_l, share_0, share_r),
        (
            six_l * (0.5 * share_l - 0.5),
            six_0 * (share_l + 0.5 * share_0 - 0.5),
            six_r * (0.5 - 0.5 * share_r),
            share_l * share_l * fraction_below,
            share_0 * share_0 * remain,
            share_r * share_r * fraction_above,
        ),
    )


def means(mixing, slope, first):
    (qm, q, qp), (sm, s, sp) = mixing, slope
    return qm + sm * first[0], q + s * first[1], qp + sp * first[2]


def carried(values, first):
    return first[3] * values[0] + first[4] * values[1] + first[5] * values[2]


def new_slope(mean, slope, second):
    total = second[0] * mean[0] + second[1] * mean[1] + second[2] * mean[2]
    return total + (second[3] * slope[0] + second[4] * slope[1] + second[5] * slope[2])


def around(value, axis):
    return lower_of(value, axis), value, upper_of(value, axis)


def kernel(
    tracers, air_mass, fluxes, inverse, source, sets, steps, out,
    raw, air, flux_in, sets_in, steps_in, matrix, source_in, gathered,
    half_x, half_y, half_air, half_flux, half_z,
    coef, coef_z, state, below, above, result,
    send_mid, send_edge, send_row, columns, work, finished, returned,
    local_sem, out_sem, flux_send, flux_recv, halo_send, halo_recv, cell_send, cell_recv, back_send, back_recv,
):
    t, l = lax.axis_index("trc"), lax.axis_index("lev")
    plane, me = lax.div(t, HALF), lax.rem(t, HALF)
    other = 1 - plane
    edge_row = (HALF - 1) * other
    own = pl.multiple_of(t * PACK, 8)
    partner = other * HALF + me

    def device(which_plane, place):
        return {"trc": which_plane * HALF + place, "lev": l}

    def put(src, dst, send, recv, to):
        pltpu.make_async_remote_copy(
            src_ref=src, dst_ref=dst, send_sem=send, recv_sem=recv, device_id=to, device_id_type=MESH
        ).start()

    def settle(ref, sem):
        pltpu.make_async_copy(ref, ref, sem).wait()

    loads = [
        pltpu.make_async_copy(fluxes, flux_in, local_sem.at[0]),
        pltpu.make_async_copy(sets, sets_in, local_sem.at[1]),
        pltpu.make_async_copy(steps, steps_in, local_sem.at[2]),
        pltpu.make_async_copy(air_mass, air, local_sem.at[3]),
        pltpu.make_async_copy(tracers, raw, local_sem.at[4]),
        pltpu.make_async_copy(source, source_in.at[pl.ds(0, SETS)], local_sem.at[5]),
    ] + [
        pltpu.make_async_copy(inverse.at[k], matrix.at[:, pl.ds(k * NT, NT)], local_sem.at[6 + k])
        for k in range(SETS)
    ]
    for load in loads:
        load.start()

    barrier = pltpu.get_barrier_semaphore()
    pl.semaphore_signal(barrier, inc=1, device_id=device(other, me), device_id_type=MESH)

    def greet(k, _):
        pl.semaphore_signal(
            barrier, inc=1, device_id=device(plane, lax.rem(me + k, HALF)), device_id_type=MESH
        )
        return 0

    lax.fori_loop(1, HALF, greet, 0)

    @pl.when(l > 0)
    def _():
        pl.semaphore_signal(barrier, inc=1, device_id={"trc": t, "lev": l - 1}, device_id_type=MESH)

    @pl.when(l < 15)
    def _():
        pl.semaphore_signal(barrier, inc=1, device_id={"trc": t, "lev": l + 1}, device_id_type=MESH)

    for load in loads[:3]:
        load.wait()
    gathered[pl.ds(own, 16), :] = jnp.concatenate(
        [flux_in[...], sets_in[...].astype(F32)], axis=0
    )
    gathered[pl.ds(own + 16, 8), :] = jnp.concatenate(
        [steps_in[...].astype(F32), jnp.zeros((4, LON), F32)], axis=0
    )

    @pl.when(l == 0)
    def _():
        below[...] = jnp.zeros_like(below)

    @pl.when(l == 15)
    def _():
        above[...] = jnp.zeros_like(above)

    pl.semaphore_wait(barrier, HALF + (l > 0).astype(jnp.int32) + (l < 15).astype(jnp.int32))

    mine = gathered.at[pl.ds(own, PACK)]
    put(mine, mine, flux_send.at[0], flux_recv.at[1], device(other, me))

    def share_own(k, _):
        put(mine, mine, flux_send.at[0], flux_recv.at[0], device(plane, lax.rem(me + k, HALF)))
        return 0

    lax.fori_loop(1, HALF, share_own, 0)
    for load in loads[3:5]:
        load.wait()
    settle(gathered.at[pl.ds(0, 15 * PACK)], flux_recv.at[0])

    lane = lax.broadcasted_iota(jnp.int32, (HALF, LON), 1)
    row = lax.broadcasted_iota(jnp.int32, (HALF, LON), 0) + plane * HALF
    first_row = pl.multiple_of(plane * HALF, HALF)
    top_level = 16 * LEV - 1

    def half_coefficients(level, _):
        def flux(direction):
            start = plane * (HALF * PACK) + direction * LEV + level
            return gathered[pl.ds(start, HALF, stride=PACK), :]

        cell_air = air[level, pl.ds(first_row, HALF), :]
        upper = jnp.where(lane < LON - 1, flux(0), 0.0)
        new_air, first, _ = coefficients(
            lower_of(cell_air, 1), cell_air, upper_of(cell_air, 1), lower_of(upper, 1), upper
        )
        for n in range(6):
            half_x[level, n] = first[n]
        upper = jnp.where(row < LAT - 1, flux(1), 0.0)
        lower = jnp.where(row > 0, lower_of(upper, 0), 0.0)
        new_air, first, _ = coefficients(
            lower_of(new_air, 0), new_air, upper_of(new_air, 0), lower, upper
        )
        for n in range(6):
            half_y[level, n] = first[n]
        half_air[level] = new_air
        half_flux[level] = flux(2)
        return 0

    lax.fori_loop(0, LEV, half_coefficients, 0)
    for level in (1, 2):
        _, first, _ = coefficients(
            half_air[level - 1], half_air[level], half_air[level + 1], half_flux[level - 1], half_flux[level]
        )
        for n in range(6):
            half_z[level - 1, n] = first[n]

    mid_rows = send_mid.reshape(HALF * 2 * 2 * TRC, LON)

    def half_tracer(n, _):
        mixing, slope = [], []
        for level in range(LEV):
            q, sx, sy, sz = (raw[level, n, f, pl.ds(first_row, HALF), :] for f in range(4))
            first = [half_x[level, i] for i in range(6)]
            q = carried(means(around(q, 1), around(sx, 1), first), first)
            sy = carried(around(sy, 1), first)
            sz = carried(around(sz, 1), first)
            first = [half_y[level, i] for i in range(6)]
            mixing.append(carried(means(around(q, 0), around(sy, 0), first), first))
            slope.append(carried(around(sz, 0), first))
        for level in (1, 2):
            first = [half_z[level - 1, i] for i in range(6)]
            q = carried(means(mixing[level - 1 : level + 2], slope[level - 1 : level + 2], first), first)
            mid_rows[pl.ds(plane * 16 + (level - 1) * TRC + n, HALF, stride=32), :] = q
        return 0

    lax.fori_loop(0, TRC, half_tracer, 0)
    my_rows = pl.ds(pl.multiple_of(t * TRC, TRC), TRC)

    def spread(first_k, which_plane, start):
        def one(k, _):
            start(which_plane, lax.rem(me + k, HALF))
            return 0

        lax.fori_loop(first_k, HALF, one, 0)

    def send_own_half(which_plane, place):
        @pl.when(place != edge_row)
        def _():
            put(
                send_mid.at[place, plane], columns.at[pl.ds(1, 2), plane, my_rows],
                cell_send.at[0], cell_recv.at[0], device(which_plane, place),
            )

    spread(0, other, send_own_half)
    spread(1, plane, send_own_half)

    theirs = gathered.at[pl.ds(pl.multiple_of(partner * PACK, 8), PACK)]
    settle(theirs, flux_recv.at[1])

    def share_partner(k, _):
        put(theirs, theirs, flux_send.at[0], flux_recv.at[2], device(plane, lax.rem(me + k, HALF)))
        return 0

    lax.fori_loop(1, HALF, share_partner, 0)
    settle(gathered.at[pl.ds(0, 15 * PACK)], flux_recv.at[2])

    lane = lax.broadcasted_iota(jnp.int32, (LAT, LON), 1)
    row = lax.broadcasted_iota(jnp.int32, (LAT, LON), 0)

    def full_coefficients(level, _):
        def flux(direction):
            return gathered[pl.ds(direction * LEV + level, LAT, stride=PACK), :]

        cell_air = air[level]
        upper = jnp.where(lane < LON - 1, flux(0), 0.0)
        new_air, first, second = coefficients(
            lower_of(cell_air, 1), cell_air, upper_of(cell_air, 1), lower_of(upper, 1), upper
        )
        for n in range(6):
            coef[level, n] = first[n]
            coef[level, 6 + n] = second[n]
        upper = jnp.where(row < LAT - 1, flux(1), 0.0)
        new_air, first, second = coefficients(
            lower_of(new_air, 0), new_air, upper_of(new_air, 0), lower_of(upper, 0), upper
        )
        for n in range(6):
            coef[level, 12 + n] = first[n]
            coef[level, 18 + n] = second[n]
        state[level, 4 * TRC] = new_air
        state[level, 4 * TRC + 1] = jnp.where(l * LEV + level < top_level, flux(2), 0.0)
        return 0

    lax.fori_loop(0, LEV, full_coefficients, 0)

    def horizontal(level):
        def tracer(n, _):
            q, sx, sy, sz = (raw[level, n, f] for f in range(4))
            first = [coef[level, i] for i in range(6)]
            second = [coef[level, 6 + i] for i in range(6)]
            slope = around(sx, 1)
            mean = means(around(q, 1), slope, first)
            q, sx = carried(mean, first), new_slope(mean, slope, second)
            sy, sz = carried(around(sy, 1), first), carried(around(sz, 1), first)
            first = [coef[level, 12 + i] for i in range(6)]
            second = [coef[level, 18 + i] for i in range(6)]
            slope = around(sy, 0)
            mean = means(around(q, 0), slope, first)
            state[level, n] = carried(mean, first)
            state[level, TRC + n] = carried(around(sz, 0), first)
            state[level, 2 * TRC + n] = carried(around(sx, 0), first)
            state[level, 3 * TRC + n] = new_slope(mean, slope, second)
            return 0

        lax.fori_loop(0, TRC, tracer, 0)

    horizontal(0)

    @pl.when(l > 0)
    def _():
        put(state.at[0], above, halo_send.at[0], halo_recv.at[0], {"trc": t, "lev": l - 1})

    horizontal(3)

    @pl.when(l < 15)
    def _():
        put(state.at[3], below, halo_send.at[1], halo_recv.at[1], {"trc": t, "lev": l + 1})

    def inner(level, _):
        horizontal(level)
        return 0

    lax.fori_loop(1, 3, inner, 0)

    edge_rows = send_edge.reshape(2 * HALF * 2 * TRC, LON)

    def vertical(level, lower_level, upper_level, keep):
        _, first, second = coefficients(
            lower_level[4 * TRC], state[level, 4 * TRC], upper_level[4 * TRC],
            lower_level[4 * TRC + 1], state[level, 4 * TRC + 1],
        )
        for i in range(6):
            coef_z[i] = first[i]
            coef_z[6 + i] = second[i]

        def tracer(n, _):
            first = [coef_z[i] for i in range(6)]
            second = [coef_z[6 + i] for i in range(6)]

            def three(f):
                return lower_level[f * TRC + n], state[level, f * TRC + n], upper_level[f * TRC + n]

            slope = three(1)
            mean = means(three(0), slope, first)
            result[level, n, 3] = new_slope(mean, slope, second)
            result[level, n, 1] = carried(three(2), first)
            result[level, n, 2] = carried(three(3), first)
            keep(n, carried(mean, first))
            return 0

        lax.fori_loop(0, TRC, tracer, 0)

    def slopes_out(level):
        return pltpu.make_async_copy(
            result.at[level, :, pl.ds(1, 3)], out.at[level, :, pl.ds(1, 3)], out_sem.at[0, level]
        )

    is_low = plane == 0
    for level in (1, 2):

        def keep_mid(n, q, level=level):
            far = jnp.where(is_low, q[HALF:], q[:HALF])
            mid_rows[pl.ds(other * 16 + (level - 1) * TRC + n, HALF, stride=32), :] = far
            near = jnp.where(is_low, q[HALF - 1 : HALF], q[HALF : HALF + 1])
            send_row[level - 1, pl.ds(n, 1), :] = near

        vertical(level, state.at[level - 1], state.at[level + 1], keep_mid)

    def send_other_half(which_plane, place):
        put(
            send_mid.at[place, other], columns.at[pl.ds(1, 2), other, my_rows],
            cell_send.at[0], cell_recv.at[0], device(which_plane, place),
        )

        @pl.when(place == edge_row)
        def _():
            put(
                send_row, columns.at[pl.ds(1, 2), plane, my_rows],
                cell_send.at[0], cell_recv.at[0], device(which_plane, place),
            )

    spread(0, other, send_other_half)
    spread(1, plane, send_other_half)
    columns[pl.ds(1, 2), other, my_rows, :] = send_mid[me, other]
    columns[pl.ds(1, 2), plane, my_rows, :] = jnp.where(
        me == edge_row, send_row[...], send_mid[me, plane]
    )
    slopes_out(1).start()
    slopes_out(2).start()

    def edge_level(which, lower_level, upper_level):
        level = 3 * which

        def keep_edge(n, q):
            for half in range(2):
                edge_rows[pl.ds(which * 256 + half * TRC + n, HALF, stride=16), :] = q[
                    half * HALF : (half + 1) * HALF
                ]

        vertical(level, lower_level, upper_level, keep_edge)

        def send_level(which_plane, place):
            put(
                send_edge.at[which, place], columns.at[level, :, my_rows],
                cell_send.at[1 + which], cell_recv.at[1 + which], device(which_plane, place),
            )

        spread(0, other, send_level)
        spread(1, plane, send_level)
        columns[level, :, my_rows, :] = send_edge[which, me]
        slopes_out(level).start()

    @pl.when(l > 0)
    def _():
        settle(below, halo_recv.at[1])

    edge_level(0, below, state.at[1])

    @pl.when(l < 15)
    def _():
        settle(above, halo_recv.at[0])

    edge_level(1, state.at[2], above)

    for load in loads[5:]:
        load.wait()
    source_in[pl.ds(4, 4), :] = jnp.zeros((4, NT), F32)
    returned_rows = returned.reshape(LEV * 2 * HALF * TRC, LON)

    def assemble(level):
        settle(returned.at[level, :, pl.ds(0, HALF - 1)], back_recv.at[level])

        def tracer(n, _):
            for half in range(2):
                start = level * 256 + half * 128 + n
                result[level, n, 0, pl.ds(half * HALF, HALF), :] = returned_rows[
                    pl.ds(start, HALF, stride=TRC), :
                ]
            return 0

        lax.fori_loop(0, TRC, tracer, 0)
        mixing_out(level).start()

    def mixing_out(level):
        return pltpu.make_async_copy(
            result.at[level, :, 0], out.at[level, :, 0], out_sem.at[1, level]
        )

    my_tracers = pl.ds(pl.multiple_of(plane * 128, 128), 128)

    def chemistry(i, _):
        level = jnp.where(i < 2, i + 1, 3 * (i - 2))

        @pl.when(i == 0)
        def _():
            settle(columns.at[pl.ds(1, 2), :, pl.ds(0, 248)], cell_recv.at[0])

        @pl.when(i == 2)
        def _():
            settle(columns.at[0, :, pl.ds(0, 248)], cell_recv.at[1])

        @pl.when(i == 3)
        def _():
            assemble(1)
            assemble(2)
            settle(columns.at[3, :, pl.ds(0, 248)], cell_recv.at[2])

        def cell_row(offset):
            return jnp.concatenate(
                [gathered[pl.ds((half * HALF + me) * PACK + offset + level, 1), :] for half in range(2)], axis=1
            )

        cell_sets, cell_steps = cell_row(12), cell_row(16)
        masks = [(cell_sets == k).astype(F32) for k in range(SETS)]
        by_set = source_in[...].T
        added = masks[0] * by_set[:, 0:1]
        for k in range(1, SETS):
            added = added + masks[k] * by_set[:, k : k + 1]
        masks = [m.astype(jnp.bfloat16) for m in masks]
        work[0] = jnp.concatenate([columns[level, 0], columns[level, 1]], axis=1)
        work[1] = added

        def step(turn, _):
            now = work[0]
            rounded = now.astype(jnp.bfloat16)
            chosen = jnp.concatenate([rounded * m for m in masks], axis=0)
            product = jnp.dot(matrix[...], chosen, preferred_element_type=F32)
            work[0] = jnp.where(turn.astype(F32) < cell_steps, product + work[1], now)
            return 0

        lax.fori_loop(0, NSTEP, step, 0)
        for half in range(2):
            finished[level, half] = work[0, my_tracers, pl.ds(half * LON, LON)]

        def send_back(which_plane, place):
            put(
                finished.at[level, :, pl.ds(pl.multiple_of(place * TRC, TRC), TRC)], returned.at[level, :, me],
                back_send.at[0], back_recv.at[level], device(which_plane, place),
            )

        spread(1, plane, send_back)
        returned[level, :, me] = finished[level, :, pl.ds(pl.multiple_of(me * TRC, TRC), TRC), :]
        return 0

    lax.fori_loop(0, LEV, chemistry, 0)
    assemble(0)
    assemble(3)

    settle(gathered.at[pl.ds(0, 31 * PACK)], flux_send.at[0])

    @pl.when(l > 0)
    def _():
        settle(above, halo_send.at[0])

    @pl.when(l < 15)
    def _():
        settle(below, halo_send.at[1])

    settle(columns.at[pl.ds(1, 2), :, pl.ds(0, 248)], cell_send.at[0])
    settle(columns.at[0, :, pl.ds(0, 248)], cell_send.at[1])
    settle(columns.at[3, :, pl.ds(0, 248)], cell_send.at[2])
    settle(returned.at[:, :, pl.ds(0, HALF - 1)], back_send.at[0])
    for level in range(LEV):
        slopes_out(level).wait()
        mixing_out(level).wait()


def on_device(tracers, air_mass, mass_flux, chem_inverse, chem_source, reaction_set, chem_steps):
    anywhere = pl.BlockSpec(memory_space=pl.ANY)
    dma, vmem = pltpu.SemaphoreType.DMA, pltpu.VMEM
    return pl.pallas_call(
        kernel,
        name="advect_and_react",
        out_shape=jax.ShapeDtypeStruct(tracers.shape, F32),
        in_specs=[anywhere] * 7,
        out_specs=anywhere,
        scratch_shapes=[
            vmem(tracers.shape, F32),
            vmem((LEV, LAT, LON), F32),
            vmem((12, LON), F32),
            vmem((LEV, LON), jnp.int32),
            vmem((LEV, LON), jnp.int32),
            vmem((NT, SETS * NT), jnp.bfloat16),
            vmem((8, NT), F32),
            vmem((LAT * PACK, LON), F32),
            vmem((LEV, 6, HALF, LON), F32),
            vmem((LEV, 6, HALF, LON), F32),
            vmem((LEV, HALF, LON), F32),
            vmem((LEV, HALF, LON), F32),
            vmem((2, 6, HALF, LON), F32),
            vmem((LEV, 24, LAT, LON), F32),
            vmem((12, LAT, LON), F32),
            vmem((LEV, 4 * TRC + 2, LAT, LON), F32),
            vmem((4 * TRC + 2, LAT, LON), F32),
            vmem((4 * TRC + 2, LAT, LON), F32),
            vmem(tracers.shape, F32),
            vmem((HALF, 2, 2, TRC, LON), F32),
            vmem((2, HALF, 2, TRC, LON), F32),
            vmem((2, TRC, LON), F32),
            vmem((LEV, 2, NT, LON), F32),
            vmem((2, NT, 2 * LON), F32),
            vmem((LEV, 2, NT // 2, LON), F32),
            vmem((LEV, 2, HALF, TRC, LON), F32),
            dma((10,)),
            dma((2, LEV)),
            dma((1,)),
            dma((3,)),
            dma((2,)),
            dma((2,)),
            dma((3,)),
            dma((3,)),
            dma((1,)),
            dma((LEV,)),
        ],
        compiler_params=pltpu.CompilerParams(
            collective_id=0, has_side_effects=True, vmem_limit_bytes=40 * 1024 * 1024
        ),
    )(
        tracers,
        air_mass,
        mass_flux.reshape(12, LON),
        chem_inverse,
        chem_source,
        reaction_set.reshape(LEV, LON),
        chem_steps.reshape(LEV, LON),
    )


def solution(mesh):
    return jax.shard_map(
        on_device,
        mesh=mesh,
        in_specs=(
            P("lev", "trc", None, None, None),
            P("lev", None, None),
            P(None, "lev", "trc", None),
            P(),
            P(),
            P("lev", "trc", None),
            P("lev", "trc", None),
        ),
        out_specs=P("lev", "trc", None, None, None),
        check_vma=False,
    )
```

```python
import jax
import jax.numpy as jnp
from jax import lax
from jax.experimental import pallas as pl
from jax.experimental.pallas import tpu as pltpu
from jax.sharding import PartitionSpec as P

MESH = pl.DeviceIdType.MESH
F32 = jnp.float32
LEV, TRC, LAT, LON = 4, 8, 32, 128
HALF = 16
NT, SETS, NSTEP = 256, 4, 6
PACK = 32


def lower_of(value, axis):
    return pltpu.roll(value, 1, axis)


def upper_of(value, axis):
    return pltpu.roll(value, value.shape[axis] - 1, axis)


def coefficients(air_below, air, air_above, lower, upper):
    from_below = jnp.maximum(lower, 0.0)
    from_above = jnp.maximum(-upper, 0.0)
    fraction_below = from_below / jnp.maximum(air_below, 0.5)
    fraction_above = from_above / jnp.maximum(air_above, 0.5)
    inverse = 1.0 / air
    out_up = jnp.maximum(upper, 0.0) * inverse
    out_down = jnp.maximum(-lower, 0.0) * inverse
    remain = 1.0 - out_down - out_up
    kept = air * remain
    new_air = from_below + kept + from_above
    inverse = 1.0 / new_air
    share_l, share_0, share_r = from_below * inverse, kept * inverse, from_above * inverse
    six_l, six_0, six_r = 6.0 * share_l, 6.0 * share_0, 6.0 * share_r
    return (
        new_air,
        (1.0 - fraction_below, out_down - out_up, fraction_above - 1.0, share_l, share_0, share_r),
        (
            six_l * (0.5 * share_l - 0.5),
            six_0 * (share_l + 0.5 * share_0 - 0.5),
            six_r * (0.5 - 0.5 * share_r),
            share_l * share_l * fraction_below,
            share_0 * share_0 * remain,
            share_r * share_r * fraction_above,
        ),
    )


def means(mixing, slope, first):
    (qm, q, qp), (sm, s, sp) = mixing, slope
    return qm + sm * first[0], q + s * first[1], qp + sp * first[2]


def carried(values, first):
    return first[3] * values[0] + first[4] * values[1] + first[5] * values[2]


def new_slope(mean, slope, second):
    total = second[0] * mean[0] + second[1] * mean[1] + second[2] * mean[2]
    return total + (second[3] * slope[0] + second[4] * slope[1] + second[5] * slope[2])


def around(value, axis):
    return lower_of(value, axis), value, upper_of(value, axis)


def kernel(
    tracers, air_mass, fluxes, inverse, source, sets, steps, out,
    raw, air, flux_in, sets_in, steps_in, matrix, source_in, gathered, pack_below, pack_above,
    quick_x, quick_y, quick_z, quick_air, quick_flux,
    coef, coef_z, state,
    send_mid, send_edge, send_row, columns, work, finished, returned,
    local_sem, flux_send, flux_recv, halo_send, halo_recv, cell_send, cell_recv, back_send, back_recv,
):
    t, l = lax.axis_index("trc"), lax.axis_index("lev")
    plane, me = lax.div(t, HALF), lax.rem(t, HALF)
    other = 1 - plane
    edge_row = (HALF - 1) * other
    own = pl.multiple_of(t * PACK, PACK)
    partner = other * HALF + me
    has_below, has_above = l > 0, l < 15

    def device(which_plane, place):
        return {"trc": which_plane * HALF + place, "lev": l}

    below, above = {"trc": t, "lev": l - 1}, {"trc": t, "lev": l + 1}

    def put(src, dst, send, recv, to):
        pltpu.make_async_remote_copy(
            src_ref=src, dst_ref=dst, send_sem=send, recv_sem=recv, device_id=to, device_id_type=MESH
        ).start()

    def settle(ref, sem):
        pltpu.make_async_copy(ref, ref, sem).wait()

    def spread(first_k, which_plane, start):
        def one(k, _):
            start(which_plane, lax.rem(me + k, HALF))
            return 0

        lax.fori_loop(first_k, HALF, one, 0)

    loads = [
        pltpu.make_async_copy(fluxes, flux_in, local_sem.at[0]),
        pltpu.make_async_copy(sets, sets_in, local_sem.at[1]),
        pltpu.make_async_copy(steps, steps_in, local_sem.at[2]),
        pltpu.make_async_copy(air_mass, air.at[pl.ds(1, LEV)], local_sem.at[3]),
        pltpu.make_async_copy(tracers, raw.at[pl.ds(1, LEV)], local_sem.at[4]),
        pltpu.make_async_copy(source, source_in.at[pl.ds(0, SETS)], local_sem.at[5]),
    ] + [
        pltpu.make_async_copy(inverse.at[k], matrix.at[:, pl.ds(k * NT, NT)], local_sem.at[6 + k])
        for k in range(SETS)
    ]
    for load in loads:
        load.start()

    barrier = pltpu.get_barrier_semaphore()

    def greet(to):
        pl.semaphore_signal(barrier, inc=1, device_id=to, device_id_type=MESH)

    greet(device(other, me))
    spread(1, plane, lambda which_plane, place: greet(device(which_plane, place)))
    pl.when(has_below)(lambda: greet(below))
    pl.when(has_above)(lambda: greet(above))

    for load in loads[:3]:
        load.wait()
    for level in range(LEV):
        for n in range(3):
            gathered[pl.ds(own + n * LEV + level, 1), :] = flux_in[n, level]
        gathered[pl.ds(own + 12 + level, 1), :] = sets_in[level].astype(F32)
        gathered[pl.ds(own + 16 + level, 1), :] = steps_in[level].astype(F32)
    gathered[pl.ds(own + 20, 4), :] = jnp.zeros((4, LON), F32)

    pl.semaphore_wait(barrier, HALF + has_below.astype(jnp.int32) + has_above.astype(jnp.int32))

    mine = gathered.at[pl.ds(own, 24)]
    short = gathered.at[pl.ds(own, 16)]
    put(mine, mine, flux_send.at[0], flux_recv.at[1], device(other, me))

    @pl.when(has_below)
    def _():
        put(short, pack_above, halo_send.at[0, 0], halo_recv.at[0, 0], below)

    @pl.when(has_above)
    def _():
        put(short, pack_below, halo_send.at[1, 0], halo_recv.at[1, 0], above)

    def share_own(which_plane, place):
        put(mine, mine, flux_send.at[0], flux_recv.at[0], device(which_plane, place))

    spread(1, plane, share_own)

    for load in loads[3:5]:
        load.wait()

    @pl.when(has_below)
    def _():
        put(raw.at[1], raw.at[LEV + 1], halo_send.at[0, 2], halo_recv.at[0, 2], below)
        put(air.at[1], air.at[LEV + 1], halo_send.at[0, 1], halo_recv.at[0, 1], below)

    @pl.when(has_above)
    def _():
        put(raw.at[LEV], raw.at[0], halo_send.at[1, 2], halo_recv.at[1, 2], above)
        put(air.at[LEV], air.at[0], halo_send.at[1, 1], halo_recv.at[1, 1], above)

    def wall(halo, pack):
        raw[halo] = jnp.zeros((TRC, 4, LAT, LON), F32)
        air[halo] = jnp.ones((LAT, LON), F32)
        pack[...] = jnp.zeros((16, LON), F32)

    pl.when(l == 0)(lambda: wall(0, pack_below))
    pl.when(l == 15)(lambda: wall(LEV + 1, pack_above))
    pl.when(has_below)(lambda: settle(pack_below, halo_recv.at[1, 0]))
    pl.when(has_above)(lambda: settle(pack_above, halo_recv.at[0, 0]))

    gathered[pl.ds(own + 24, 8), :] = jnp.concatenate(
        [pack_below[n * LEV + 3 : n * LEV + 4, :] for n in range(3)]
        + [pack_above[n * LEV : n * LEV + 1, :] for n in range(3)]
        + [jnp.zeros((2, LON), F32)],
        axis=0,
    )
    near = gathered.at[pl.ds(own + 24, 8)]
    put(near, near, flux_send.at[0], flux_recv.at[4], device(other, me))

    def share_near(which_plane, place):
        put(near, near, flux_send.at[0], flux_recv.at[2], device(which_plane, place))

    spread(1, plane, share_near)
    settle(gathered.at[pl.ds(0, 15 * 24)], flux_recv.at[0])

    top_level = 16 * LEV - 1
    mid_rows = send_mid.reshape(HALF * 2 * 2 * TRC, LON)
    edge_rows = send_edge.reshape(2 * HALF * 2 * TRC, LON)
    my_rows = pl.ds(pl.multiple_of(t * TRC, TRC), TRC)

    def quick(start, count, keep):
        rows, some = pl.ds(start, count), pl.ds(0, count)
        lane = lax.broadcasted_iota(jnp.int32, (count, LON), 1)
        row = lax.broadcasted_iota(jnp.int32, (count, LON), 0) + start

        def prepare(level, _):
            def flux(direction):
                return gathered[pl.ds(start * PACK + direction * LEV + level, count, stride=PACK), :]

            cell_air = air[1 + level, rows, :]
            upper = jnp.where(lane < LON - 1, flux(0), 0.0)
            new_air, first, _ = coefficients(
                lower_of(cell_air, 1), cell_air, upper_of(cell_air, 1), lower_of(upper, 1), upper
            )
            for n in range(6):
                quick_x[level, n, some] = first[n]
            upper = jnp.where(row < LAT - 1, flux(1), 0.0)
            lower = jnp.where(row > 0, lower_of(upper, 0), 0.0)
            new_air, first, _ = coefficients(
                lower_of(new_air, 0), new_air, upper_of(new_air, 0), lower, upper
            )
            for n in range(6):
                quick_y[level, n, some] = first[n]
            quick_air[level, some] = new_air
            quick_flux[level, some] = flux(2)
            return 0

        lax.fori_loop(0, LEV, prepare, 0)
        for level in (1, 2):
            _, first, _ = coefficients(
                quick_air[level - 1, some], quick_air[level, some], quick_air[level + 1, some],
                quick_flux[level - 1, some], quick_flux[level, some],
            )
            for n in range(6):
                quick_z[level - 1, n, some] = first[n]

        def tracer(n, _):
            mixing, slope = [], []
            for level in range(LEV):
                q, sx, sy, sz = (raw[1 + level, n, f, rows, :] for f in range(4))
                first = [quick_x[level, i, some] for i in range(6)]
                q = carried(means(around(q, 1), around(sx, 1), first), first)
                sy = carried(around(sy, 1), first)
                sz = carried(around(sz, 1), first)
                first = [quick_y[level, i, some] for i in range(6)]
                mixing.append(carried(means(around(q, 0), around(sy, 0), first), first))
                slope.append(carried(around(sz, 0), first))
            for level in (1, 2):
                first = [quick_z[level - 1, i, some] for i in range(6)]
                three = slice(level - 1, level + 2)
                keep(n, level - 1, carried(means(mixing[three], slope[three], first), first))
            return 0

        lax.fori_loop(0, TRC, tracer, 0)

    def keep_own_half(n, level, q):
        mid_rows[pl.ds(plane * 16 + level * TRC + n, HALF, stride=32), :] = q

    quick(pl.multiple_of(plane * HALF, HALF), HALF, keep_own_half)

    def send_own_half(which_plane, place):
        @pl.when(place != edge_row)
        def _():
            put(
                send_mid.at[place, plane], columns.at[pl.ds(1, 2), plane, my_rows],
                cell_send.at[0], cell_recv.at[0], device(which_plane, place),
            )

    spread(0, other, send_own_half)
    spread(1, plane, send_own_half)

    theirs = gathered.at[pl.ds(pl.multiple_of(partner * PACK, PACK), 24)]
    settle(theirs, flux_recv.at[1])

    def share_partner(which_plane, place):
        put(theirs, theirs, flux_send.at[0], flux_recv.at[3], device(which_plane, place))

    spread(1, plane, share_partner)
    settle(gathered.at[pl.ds(0, 15 * 24)], flux_recv.at[3])

    is_low = plane == 0

    def keep_other_half(n, level, q):
        far = jnp.where(is_low, q[HALF:], q[:HALF])
        mid_rows[pl.ds(other * 16 + level * TRC + n, HALF, stride=32), :] = far
        send_row[level, pl.ds(n, 1), :] = jnp.where(is_low, q[HALF - 1 : HALF], q[HALF : HALF + 1])

    quick(0, LAT, keep_other_half)

    def send_other_half(which_plane, place):
        put(
            send_mid.at[place, other], columns.at[pl.ds(1, 2), other, my_rows],
            cell_send.at[0], cell_recv.at[0], device(which_plane, place),
        )

        @pl.when(place == edge_row)
        def _():
            put(
                send_row, columns.at[pl.ds(1, 2), plane, my_rows],
                cell_send.at[0], cell_recv.at[0], device(which_plane, place),
            )

    spread(0, other, send_other_half)
    spread(1, plane, send_other_half)
    columns[pl.ds(1, 2), other, my_rows, :] = send_mid[me, other]
    columns[pl.ds(1, 2), plane, my_rows, :] = jnp.where(
        me == edge_row, send_row[...], send_mid[me, plane]
    )

    their_near = gathered.at[pl.ds(pl.multiple_of(partner * PACK + 24, 8), 8)]
    settle(their_near, flux_recv.at[4])

    def share_their_near(which_plane, place):
        put(their_near, their_near, flux_send.at[0], flux_recv.at[5], device(which_plane, place))

    spread(1, plane, share_their_near)

    lane = lax.broadcasted_iota(jnp.int32, (LAT, LON), 1)
    row = lax.broadcasted_iota(jnp.int32, (LAT, LON), 0)

    def horizontal(level, _):
        def flux(direction):
            inside = direction * LEV + level - 1
            place = jnp.where(level == 0, 24 + direction, jnp.where(level == LEV + 1, 27 + direction, inside))
            return gathered[pl.ds(place, LAT, stride=PACK), :]

        cell_air = air[level]
        upper = jnp.where(lane < LON - 1, flux(0), 0.0)
        new_air, first, second = coefficients(
            lower_of(cell_air, 1), cell_air, upper_of(cell_air, 1), lower_of(upper, 1), upper
        )
        for n in range(6):
            coef[n] = first[n]
            coef[6 + n] = second[n]
        upper = jnp.where(row < LAT - 1, flux(1), 0.0)
        new_air, first, second = coefficients(
            lower_of(new_air, 0), new_air, upper_of(new_air, 0), lower_of(upper, 0), upper
        )
        for n in range(6):
            coef[12 + n] = first[n]
            coef[18 + n] = second[n]
        state[level, 4 * TRC] = new_air
        state[level, 4 * TRC + 1] = jnp.where(l * LEV + level - 1 < top_level, flux(2), 0.0)

        def tracer(n, _):
            q, sx, sy, sz = (raw[level, n, f] for f in range(4))
            first = [coef[i] for i in range(6)]
            second = [coef[6 + i] for i in range(6)]
            slope = around(sx, 1)
            mean = means(around(q, 1), slope, first)
            q, sx = carried(mean, first), new_slope(mean, slope, second)
            sy, sz = carried(around(sy, 1), first), carried(around(sz, 1), first)
            first = [coef[12 + i] for i in range(6)]
            second = [coef[18 + i] for i in range(6)]
            slope = around(sy, 0)
            mean = means(around(q, 0), slope, first)
            state[level, n] = carried(mean, first)
            state[level, TRC + n] = carried(around(sz, 0), first)
            state[level, 2 * TRC + n] = carried(around(sx, 0), first)
            state[level, 3 * TRC + n] = new_slope(mean, slope, second)
            return 0

        lax.fori_loop(0, TRC, tracer, 0)
        return 0

    lax.fori_loop(1, LEV + 1, horizontal, 0)

    def vertical(level):
        at = level + 1
        _, first, second = coefficients(
            state[at - 1, 4 * TRC], state[at, 4 * TRC], state[at + 1, 4 * TRC],
            state[at - 1, 4 * TRC + 1], state[at, 4 * TRC + 1],
        )
        for i in range(6):
            coef_z[i] = first[i]
            coef_z[6 + i] = second[i]

        def tracer(n, _):
            first = [coef_z[i] for i in range(6)]
            second = [coef_z[6 + i] for i in range(6)]

            def three(f):
                return [state[at + k, f * TRC + n] for k in (-1, 0, 1)]

            slope = three(1)
            mean = means(three(0), slope, first)
            out[level, n, 0] = carried(mean, first)
            out[level, n, 3] = new_slope(mean, slope, second)
            out[level, n, 1] = carried(three(2), first)
            out[level, n, 2] = carried(three(3), first)
            return 0

        lax.fori_loop(0, TRC, tracer, 0)

    def inner_level(level, _):
        vertical(level)
        return 0

    lax.fori_loop(1, 3, inner_level, 0)

    settle(gathered.at[pl.ds(0, 15 * 8)], flux_recv.at[2])
    settle(gathered.at[pl.ds(0, 15 * 8)], flux_recv.at[5])

    @pl.when(has_below)
    def _():
        settle(air.at[0], halo_recv.at[1, 1])
        settle(raw.at[0], halo_recv.at[1, 2])

    @pl.when(has_above)
    def _():
        settle(air.at[LEV + 1], halo_recv.at[0, 1])
        settle(raw.at[LEV + 1], halo_recv.at[0, 2])

    def outer_level(i, _):
        return horizontal(i * (LEV + 1), 0)

    lax.fori_loop(0, 2, outer_level, 0)

    def edge_level(which, _):
        level = 3 * which
        vertical(level)

        def keep(n, _):
            for half in range(2):
                edge_rows[pl.ds(which * 256 + half * TRC + n, HALF, stride=16), :] = out[
                    level, n, 0, pl.ds(half * HALF, HALF), :
                ]
            return 0

        lax.fori_loop(0, TRC, keep, 0)

        def send_level(which_plane, place):
            put(
                send_edge.at[which, place], columns.at[level, :, my_rows],
                cell_send.at[1 + which], cell_recv.at[1 + which], device(which_plane, place),
            )

        spread(0, other, send_level)
        spread(1, plane, send_level)
        columns[level, :, my_rows, :] = send_edge[which, me]
        return 0

    lax.fori_loop(0, 2, edge_level, 0)

    for load in loads[5:]:
        load.wait()
    source_in[pl.ds(4, 4), :] = jnp.zeros((4, NT), F32)
    returned_rows = returned.reshape(LEV * 2 * HALF * TRC, LON)

    def assemble(level):
        settle(returned.at[level, :, pl.ds(0, HALF - 1)], back_recv.at[level])

        def tracer(n, _):
            for half in range(2):
                start = level * 256 + half * 128 + n
                out[level, n, 0, pl.ds(half * HALF, HALF), :] = returned_rows[
                    pl.ds(start, HALF, stride=TRC), :
                ]
            return 0

        lax.fori_loop(0, TRC, tracer, 0)

    my_tracers = pl.ds(pl.multiple_of(plane * 128, 128), 128)

    def chemistry(i, _):
        level = jnp.where(i < 2, i + 1, 3 * (i - 2))

        @pl.when(i == 0)
        def _():
            settle(columns.at[pl.ds(1, 2), :, pl.ds(0, 248)], cell_recv.at[0])

        @pl.when(i == 2)
        def _():
            settle(columns.at[0, :, pl.ds(0, 248)], cell_recv.at[1])

        @pl.when(i == 3)
        def _():
            assemble(1)
            assemble(2)
            settle(columns.at[3, :, pl.ds(0, 248)], cell_recv.at[2])

        def cell_row(offset):
            return jnp.concatenate(
                [gathered[pl.ds((half * HALF + me) * PACK + offset + level, 1), :] for half in range(2)], axis=1
            )

        cell_sets, cell_steps = cell_row(12), cell_row(16)
        masks = [(cell_sets == k).astype(F32) for k in range(SETS)]
        by_set = source_in[...].T
        added = masks[0] * by_set[:, 0:1]
        for k in range(1, SETS):
            added = added + masks[k] * by_set[:, k : k + 1]
        masks = [m.astype(jnp.bfloat16) for m in masks]
        work[0] = jnp.concatenate([columns[level, 0], columns[level, 1]], axis=1)
        work[1] = added

        def step(turn, _):
            now = work[0]
            rounded = now.astype(jnp.bfloat16)
            chosen = jnp.concatenate([rounded * m for m in masks], axis=0)
            product = jnp.dot(matrix[...], chosen, preferred_element_type=F32)
            work[0] = jnp.where(turn.astype(F32) < cell_steps, product + work[1], now)
            return 0

        lax.fori_loop(0, NSTEP, step, 0)
        for half in range(2):
            finished[level, half] = work[0, my_tracers, pl.ds(half * LON, LON)]

        def send_back(which_plane, place):
            put(
                finished.at[level, :, pl.ds(pl.multiple_of(place * TRC, TRC), TRC)], returned.at[level, :, me],
                back_send.at[0], back_recv.at[level], device(which_plane, place),
            )

        spread(1, plane, send_back)
        returned[level, :, me] = finished[level, :, pl.ds(pl.multiple_of(me * TRC, TRC), TRC), :]
        return 0

    lax.fori_loop(0, LEV, chemistry, 0)
    assemble(0)
    assemble(3)

    settle(gathered.at[pl.ds(0, 31 * PACK)], flux_send.at[0])

    def halo_sent(side):
        settle(pack_below, halo_send.at[side, 0])
        settle(air.at[0], halo_send.at[side, 1])
        settle(raw.at[0], halo_send.at[side, 2])

    pl.when(has_below)(lambda: halo_sent(0))
    pl.when(has_above)(lambda: halo_sent(1))
    settle(columns.at[pl.ds(1, 2), :, pl.ds(0, 248)], cell_send.at[0])
    settle(columns.at[0, :, pl.ds(0, 248)], cell_send.at[1])
    settle(columns.at[3, :, pl.ds(0, 248)], cell_send.at[2])
    settle(returned.at[:, :, pl.ds(0, HALF - 1)], back_send.at[0])


def on_device(tracers, air_mass, mass_flux, chem_inverse, chem_source, reaction_set, chem_steps):
    hbm = pl.BlockSpec(memory_space=pltpu.HBM)
    dma, vmem = pltpu.SemaphoreType.DMA, pltpu.VMEM
    return pl.pallas_call(
        kernel,
        name="advect_and_react",
        out_shape=pltpu.VMEM(tracers.shape, F32),
        in_specs=[hbm] * 7,
        out_specs=pl.BlockSpec(memory_space=pltpu.VMEM),
        scratch_shapes=[
            vmem((LEV + 2,) + tracers.shape[1:], F32),
            vmem((LEV + 2, LAT, LON), F32),
            vmem(mass_flux.shape, F32),
            vmem(reaction_set.shape, jnp.int32),
            vmem(chem_steps.shape, jnp.int32),
            vmem((NT, SETS * NT), jnp.bfloat16),
            vmem((8, NT), F32),
            vmem((LAT * PACK, LON), F32),
            vmem((16, LON), F32),
            vmem((16, LON), F32),
            vmem((LEV, 6, LAT, LON), F32),
            vmem((LEV, 6, LAT, LON), F32),
            vmem((2, 6, LAT, LON), F32),
            vmem((LEV, LAT, LON), F32),
            vmem((LEV, LAT, LON), F32),
            vmem((24, LAT, LON), F32),
            vmem((12, LAT, LON), F32),
            vmem((LEV + 2, 4 * TRC + 2, LAT, LON), F32),
            vmem((HALF, 2, 2, TRC, LON), F32),
            vmem((2, HALF, 2, TRC, LON), F32),
            vmem((2, TRC, LON), F32),
            vmem((LEV, 2, NT, LON), F32),
            vmem((2, NT, 2 * LON), F32),
            vmem((LEV, 2, NT // 2, LON), F32),
            vmem((LEV, 2, HALF, TRC, LON), F32),
            dma((10,)),
            dma((1,)),
            dma((6,)),
            dma((2, 3)),
            dma((2, 3)),
            dma((3,)),
            dma((3,)),
            dma((1,)),
            dma((LEV,)),
        ],
        compiler_params=pltpu.CompilerParams(
            collective_id=0, has_side_effects=True, vmem_limit_bytes=40 * 1024 * 1024
        ),
    )(
        *(
            pltpu.with_memory_space_constraint(value, pltpu.HBM)
            for value in (
                tracers, air_mass, mass_flux, chem_inverse, chem_source, reaction_set, chem_steps
            )
        )
    )


def solution(mesh):
    return jax.shard_map(
        on_device,
        mesh=mesh,
        in_specs=(
            P("lev", "trc", None, None, None),
            P("lev", None, None),
            P(None, "lev", "trc", None),
            P(),
            P(),
            P("lev", "trc", None),
            P("lev", "trc", None),
        ),
        out_specs=P("lev", "trc", None, None, None),
        check_vma=False,
    )
```

```python
import jax
import jax.numpy as jnp
from jax import lax
from jax.experimental import pallas as pl
from jax.experimental.pallas import tpu as pltpu
from jax.sharding import PartitionSpec as P

MESH = pl.DeviceIdType.MESH
F32 = jnp.float32
LEV, TRC, LAT, LON = 4, 8, 32, 128
HALF = 16
NT, SETS, NSTEP = 256, 4, 6
PACK = 32


def lower_of(value, axis):
    return pltpu.roll(value, 1, axis)


def upper_of(value, axis):
    return pltpu.roll(value, value.shape[axis] - 1, axis)


def coefficients(air_below, air, air_above, lower, upper):
    from_below = jnp.maximum(lower, 0.0)
    from_above = jnp.maximum(-upper, 0.0)
    fraction_below = from_below / jnp.maximum(air_below, 0.5)
    fraction_above = from_above / jnp.maximum(air_above, 0.5)
    inverse = 1.0 / air
    out_up = jnp.maximum(upper, 0.0) * inverse
    out_down = jnp.maximum(-lower, 0.0) * inverse
    remain = 1.0 - out_down - out_up
    kept = air * remain
    new_air = from_below + kept + from_above
    inverse = 1.0 / new_air
    share_l, share_0, share_r = from_below * inverse, kept * inverse, from_above * inverse
    six_l, six_0, six_r = 6.0 * share_l, 6.0 * share_0, 6.0 * share_r
    return (
        new_air,
        (1.0 - fraction_below, out_down - out_up, fraction_above - 1.0, share_l, share_0, share_r),
        (
            six_l * (0.5 * share_l - 0.5),
            six_0 * (share_l + 0.5 * share_0 - 0.5),
            six_r * (0.5 - 0.5 * share_r),
            share_l * share_l * fraction_below,
            share_0 * share_0 * remain,
            share_r * share_r * fraction_above,
        ),
    )


def means(mixing, slope, first):
    (qm, q, qp), (sm, s, sp) = mixing, slope
    return qm + sm * first[0], q + s * first[1], qp + sp * first[2]


def carried(values, first):
    return first[3] * values[0] + first[4] * values[1] + first[5] * values[2]


def new_slope(mean, slope, second):
    total = second[0] * mean[0] + second[1] * mean[1] + second[2] * mean[2]
    return total + (second[3] * slope[0] + second[4] * slope[1] + second[5] * slope[2])


def around(value, axis):
    return lower_of(value, axis), value, upper_of(value, axis)


def kernel(
    tracers, air_mass, fluxes, inverse, source, sets, steps, out,
    raw, air, flux_in, sets_in, steps_in, matrix, source_in, gathered, pack_below, pack_above,
    quick_x, quick_y, quick_z, quick_air, quick_flux,
    coef, coef_z, state,
    send_mid, send_edge, send_row, columns, work, finished, returned,
    local_sem, flux_send, flux_recv, halo_send, halo_recv, cell_send, cell_recv, back_send, back_recv,
):
    t, l = lax.axis_index("trc"), lax.axis_index("lev")
    plane, me = lax.div(t, HALF), lax.rem(t, HALF)
    other = 1 - plane
    edge_row = (HALF - 1) * other
    own = pl.multiple_of(t * PACK, PACK)
    partner = other * HALF + me
    has_below, has_above = l > 0, l < 15

    def device(which_plane, place):
        return {"trc": which_plane * HALF + place, "lev": l}

    below, above = {"trc": t, "lev": l - 1}, {"trc": t, "lev": l + 1}

    def put(src, dst, send, recv, to):
        pltpu.make_async_remote_copy(
            src_ref=src, dst_ref=dst, send_sem=send, recv_sem=recv, device_id=to, device_id_type=MESH
        ).start()

    def settle(ref, sem):
        pltpu.make_async_copy(ref, ref, sem).wait()

    def spread(first_k, which_plane, start):
        def one(k, _):
            start(which_plane, lax.rem(me + k, HALF))
            return 0

        lax.fori_loop(first_k, HALF, one, 0)

    loads = [
        pltpu.make_async_copy(fluxes, flux_in, local_sem.at[0]),
        pltpu.make_async_copy(sets, sets_in, local_sem.at[1]),
        pltpu.make_async_copy(steps, steps_in, local_sem.at[2]),
        pltpu.make_async_copy(air_mass, air.at[pl.ds(1, LEV)], local_sem.at[3]),
        pltpu.make_async_copy(tracers, raw.at[pl.ds(1, LEV)], local_sem.at[4]),
        pltpu.make_async_copy(source, source_in.at[pl.ds(0, SETS)], local_sem.at[5]),
    ] + [
        pltpu.make_async_copy(inverse.at[k], matrix.at[:, pl.ds(k * NT, NT)], local_sem.at[6 + k])
        for k in range(SETS)
    ]
    for load in loads:
        load.start()

    barrier = pltpu.get_barrier_semaphore()

    def greet(to):
        pl.semaphore_signal(barrier, inc=1, device_id=to, device_id_type=MESH)

    greet(device(other, me))
    spread(1, plane, lambda which_plane, place: greet(device(which_plane, place)))
    pl.when(has_below)(lambda: greet(below))
    pl.when(has_above)(lambda: greet(above))

    for load in loads[:3]:
        load.wait()
    for level in range(LEV):
        for n in range(3):
            gathered[pl.ds(own + n * LEV + level, 1), :] = flux_in[n, level]
        gathered[pl.ds(own + 12 + level, 1), :] = sets_in[level].astype(F32)
        gathered[pl.ds(own + 16 + level, 1), :] = steps_in[level].astype(F32)
    gathered[pl.ds(own + 20, 4), :] = jnp.zeros((4, LON), F32)

    pl.semaphore_wait(barrier, HALF + has_below.astype(jnp.int32) + has_above.astype(jnp.int32))

    mine = gathered.at[pl.ds(own, 24)]
    short = gathered.at[pl.ds(own, 16)]
    put(mine, mine, flux_send.at[0], flux_recv.at[1], device(other, me))

    @pl.when(has_below)
    def _():
        put(short, pack_above, halo_send.at[0, 0], halo_recv.at[0, 0], below)

    @pl.when(has_above)
    def _():
        put(short, pack_below, halo_send.at[1, 0], halo_recv.at[1, 0], above)

    def share_own(which_plane, place):
        put(mine, mine, flux_send.at[0], flux_recv.at[0], device(which_plane, place))

    spread(1, plane, share_own)

    for load in loads[3:5]:
        load.wait()

    @pl.when(has_below)
    def _():
        put(raw.at[1], raw.at[LEV + 1], halo_send.at[0, 2], halo_recv.at[0, 2], below)
        put(air.at[1], air.at[LEV + 1], halo_send.at[0, 1], halo_recv.at[0, 1], below)

    @pl.when(has_above)
    def _():
        put(raw.at[LEV], raw.at[0], halo_send.at[1, 2], halo_recv.at[1, 2], above)
        put(air.at[LEV], air.at[0], halo_send.at[1, 1], halo_recv.at[1, 1], above)

    def wall(halo, pack):
        raw[halo] = jnp.zeros((TRC, 4, LAT, LON), F32)
        air[halo] = jnp.ones((LAT, LON), F32)
        pack[...] = jnp.zeros((16, LON), F32)

    pl.when(l == 0)(lambda: wall(0, pack_below))
    pl.when(l == 15)(lambda: wall(LEV + 1, pack_above))
    pl.when(has_below)(lambda: settle(pack_below, halo_recv.at[1, 0]))
    pl.when(has_above)(lambda: settle(pack_above, halo_recv.at[0, 0]))

    gathered[pl.ds(own + 24, 8), :] = jnp.concatenate(
        [pack_below[n * LEV + 3 : n * LEV + 4, :] for n in range(3)]
        + [pack_above[n * LEV : n * LEV + 1, :] for n in range(3)]
        + [jnp.zeros((2, LON), F32)],
        axis=0,
    )
    near = gathered.at[pl.ds(own + 24, 8)]
    put(near, near, flux_send.at[0], flux_recv.at[4], device(other, me))

    def share_near(which_plane, place):
        put(near, near, flux_send.at[0], flux_recv.at[2], device(which_plane, place))

    spread(1, plane, share_near)
    settle(gathered.at[pl.ds(0, 15 * 24)], flux_recv.at[0])

    top_level = 16 * LEV - 1
    mid_rows = send_mid.reshape(HALF * 2 * 2 * TRC, LON)
    edge_rows = send_edge.reshape(2 * HALF * 2 * TRC, LON)
    my_rows = pl.ds(pl.multiple_of(t * TRC, TRC), TRC)

    def quick(start, count, keep):
        rows, some = pl.ds(start, count), pl.ds(0, count)
        lane = lax.broadcasted_iota(jnp.int32, (count, LON), 1)
        row = lax.broadcasted_iota(jnp.int32, (count, LON), 0) + start

        def prepare(level, _):
            def flux(direction):
                return gathered[pl.ds(start * PACK + direction * LEV + level, count, stride=PACK), :]

            cell_air = air[1 + level, rows, :]
            upper = jnp.where(lane < LON - 1, flux(0), 0.0)
            new_air, first, _ = coefficients(
                lower_of(cell_air, 1), cell_air, upper_of(cell_air, 1), lower_of(upper, 1), upper
            )
            for n in range(6):
                quick_x[level, n, some] = first[n]
            upper = jnp.where(row < LAT - 1, flux(1), 0.0)
            lower = jnp.where(row > 0, lower_of(upper, 0), 0.0)
            new_air, first, _ = coefficients(
                lower_of(new_air, 0), new_air, upper_of(new_air, 0), lower, upper
            )
            for n in range(6):
                quick_y[level, n, some] = first[n]
            quick_air[level, some] = new_air
            quick_flux[level, some] = flux(2)
            return 0

        lax.fori_loop(0, LEV, prepare, 0, unroll=2 if count == HALF else 1)
        for level in (1, 2):
            _, first, _ = coefficients(
                quick_air[level - 1, some], quick_air[level, some], quick_air[level + 1, some],
                quick_flux[level - 1, some], quick_flux[level, some],
            )
            for n in range(6):
                quick_z[level - 1, n, some] = first[n]

        def tracer(n, _):
            mixing, slope = [], []
            for level in range(LEV):
                q, sx, sy, sz = (raw[1 + level, n, f, rows, :] for f in range(4))
                first = [quick_x[level, i, some] for i in range(6)]
                q = carried(means(around(q, 1), around(sx, 1), first), first)
                sy = carried(around(sy, 1), first)
                sz = carried(around(sz, 1), first)
                first = [quick_y[level, i, some] for i in range(6)]
                mixing.append(carried(means(around(q, 0), around(sy, 0), first), first))
                slope.append(carried(around(sz, 0), first))
            for level in (1, 2):
                first = [quick_z[level - 1, i, some] for i in range(6)]
                three = slice(level - 1, level + 2)
                keep(n, level - 1, carried(means(mixing[three], slope[three], first), first))
            return 0

        lax.fori_loop(0, TRC, tracer, 0, unroll=2 if count == HALF else 1)

    def keep_own_half(n, level, q):
        mid_rows[pl.ds(plane * 16 + level * TRC + n, HALF, stride=32), :] = q

    quick(pl.multiple_of(plane * HALF, HALF), HALF, keep_own_half)

    def send_own_half(which_plane, place):
        @pl.when(place != edge_row)
        def _():
            put(
                send_mid.at[place, plane], columns.at[pl.ds(1, 2), plane, my_rows],
                cell_send.at[0], cell_recv.at[0], device(which_plane, place),
            )

    spread(0, other, send_own_half)
    spread(1, plane, send_own_half)

    theirs = gathered.at[pl.ds(pl.multiple_of(partner * PACK, PACK), 24)]
    settle(theirs, flux_recv.at[1])

    def share_partner(which_plane, place):
        put(theirs, theirs, flux_send.at[0], flux_recv.at[3], device(which_plane, place))

    spread(1, plane, share_partner)
    settle(gathered.at[pl.ds(0, 15 * 24)], flux_recv.at[3])

    is_low = plane == 0

    def keep_other_half(n, level, q):
        far = jnp.where(is_low, q[HALF:], q[:HALF])
        mid_rows[pl.ds(other * 16 + level * TRC + n, HALF, stride=32), :] = far
        send_row[level, pl.ds(n, 1), :] = jnp.where(is_low, q[HALF - 1 : HALF], q[HALF : HALF + 1])

    quick(0, LAT, keep_other_half)

    def send_other_half(which_plane, place):
        put(
            send_mid.at[place, other], columns.at[pl.ds(1, 2), other, my_rows],
            cell_send.at[0], cell_recv.at[0], device(which_plane, place),
        )

        @pl.when(place == edge_row)
        def _():
            put(
                send_row, columns.at[pl.ds(1, 2), plane, my_rows],
                cell_send.at[0], cell_recv.at[0], device(which_plane, place),
            )

    spread(0, other, send_other_half)
    spread(1, plane, send_other_half)
    columns[pl.ds(1, 2), other, my_rows, :] = send_mid[me, other]
    columns[pl.ds(1, 2), plane, my_rows, :] = jnp.where(
        me == edge_row, send_row[...], send_mid[me, plane]
    )

    their_near = gathered.at[pl.ds(pl.multiple_of(partner * PACK + 24, 8), 8)]
    settle(their_near, flux_recv.at[4])

    def share_their_near(which_plane, place):
        put(their_near, their_near, flux_send.at[0], flux_recv.at[5], device(which_plane, place))

    spread(1, plane, share_their_near)

    lane = lax.broadcasted_iota(jnp.int32, (LAT, LON), 1)
    row = lax.broadcasted_iota(jnp.int32, (LAT, LON), 0)

    def horizontal(level, _):
        def flux(direction):
            inside = direction * LEV + level - 1
            place = jnp.where(level == 0, 24 + direction, jnp.where(level == LEV + 1, 27 + direction, inside))
            return gathered[pl.ds(place, LAT, stride=PACK), :]

        cell_air = air[level]
        upper = jnp.where(lane < LON - 1, flux(0), 0.0)
        new_air, first, second = coefficients(
            lower_of(cell_air, 1), cell_air, upper_of(cell_air, 1), lower_of(upper, 1), upper
        )
        for n in range(6):
            coef[n] = first[n]
            coef[6 + n] = second[n]
        upper = jnp.where(row < LAT - 1, flux(1), 0.0)
        new_air, first, second = coefficients(
            lower_of(new_air, 0), new_air, upper_of(new_air, 0), lower_of(upper, 0), upper
        )
        for n in range(6):
            coef[12 + n] = first[n]
            coef[18 + n] = second[n]
        state[level, 4 * TRC] = new_air
        state[level, 4 * TRC + 1] = jnp.where(l * LEV + level - 1 < top_level, flux(2), 0.0)

        def tracer(n, _):
            q, sx, sy, sz = (raw[level, n, f] for f in range(4))
            first = [coef[i] for i in range(6)]
            second = [coef[6 + i] for i in range(6)]
            slope = around(sx, 1)
            mean = means(around(q, 1), slope, first)
            q, sx = carried(mean, first), new_slope(mean, slope, second)
            sy, sz = carried(around(sy, 1), first), carried(around(sz, 1), first)
            first = [coef[12 + i] for i in range(6)]
            second = [coef[18 + i] for i in range(6)]
            slope = around(sy, 0)
            mean = means(around(q, 0), slope, first)
            state[level, n] = carried(mean, first)
            state[level, TRC + n] = carried(around(sz, 0), first)
            state[level, 2 * TRC + n] = carried(around(sx, 0), first)
            state[level, 3 * TRC + n] = new_slope(mean, slope, second)
            return 0

        lax.fori_loop(0, TRC, tracer, 0)
        return 0

    lax.fori_loop(1, LEV + 1, horizontal, 0)

    def vertical(level):
        at = level + 1
        _, first, second = coefficients(
            state[at - 1, 4 * TRC], state[at, 4 * TRC], state[at + 1, 4 * TRC],
            state[at - 1, 4 * TRC + 1], state[at, 4 * TRC + 1],
        )
        for i in range(6):
            coef_z[i] = first[i]
            coef_z[6 + i] = second[i]

        def tracer(n, _):
            first = [coef_z[i] for i in range(6)]
            second = [coef_z[6 + i] for i in range(6)]

            def three(f):
                return [state[at + k, f * TRC + n] for k in (-1, 0, 1)]

            slope = three(1)
            mean = means(three(0), slope, first)
            out[level, n, 0] = carried(mean, first)
            out[level, n, 3] = new_slope(mean, slope, second)
            out[level, n, 1] = carried(three(2), first)
            out[level, n, 2] = carried(three(3), first)
            return 0

        lax.fori_loop(0, TRC, tracer, 0)

    def inner_level(level, _):
        vertical(level)
        return 0

    lax.fori_loop(1, 3, inner_level, 0)

    settle(gathered.at[pl.ds(0, 15 * 8)], flux_recv.at[2])
    settle(gathered.at[pl.ds(0, 15 * 8)], flux_recv.at[5])

    @pl.when(has_below)
    def _():
        settle(air.at[0], halo_recv.at[1, 1])
        settle(raw.at[0], halo_recv.at[1, 2])

    @pl.when(has_above)
    def _():
        settle(air.at[LEV + 1], halo_recv.at[0, 1])
        settle(raw.at[LEV + 1], halo_recv.at[0, 2])

    def outer_level(i, _):
        return horizontal(i * (LEV + 1), 0)

    lax.fori_loop(0, 2, outer_level, 0)

    def edge_level(which, _):
        level = 3 * which
        vertical(level)

        def keep(n, _):
            for half in range(2):
                edge_rows[pl.ds(which * 256 + half * TRC + n, HALF, stride=16), :] = out[
                    level, n, 0, pl.ds(half * HALF, HALF), :
                ]
            return 0

        lax.fori_loop(0, TRC, keep, 0)

        def send_level(which_plane, place):
            put(
                send_edge.at[which, place], columns.at[level, :, my_rows],
                cell_send.at[1 + which], cell_recv.at[1 + which], device(which_plane, place),
            )

        spread(0, other, send_level)
        spread(1, plane, send_level)
        columns[level, :, my_rows, :] = send_edge[which, me]
        return 0

    pace = lax.div(l, 2)
    held = (pace == 5) | (pace == 6)

    @pl.when(held)
    def _():
        settle(columns.at[pl.ds(1, 2), :, pl.ds(0, 248)], cell_recv.at[0])

    lax.fori_loop(0, 2, edge_level, 0)

    for load in loads[5:]:
        load.wait()
    source_in[pl.ds(4, 4), :] = jnp.zeros((4, NT), F32)
    returned_rows = returned.reshape(LEV * 2 * HALF * TRC, LON)

    def assemble(level):
        settle(returned.at[level, :, pl.ds(0, HALF - 1)], back_recv.at[level])

        def tracer(n, _):
            for half in range(2):
                start = level * 256 + half * 128 + n
                out[level, n, 0, pl.ds(half * HALF, HALF), :] = returned_rows[
                    pl.ds(start, HALF, stride=TRC), :
                ]
            return 0

        lax.fori_loop(0, TRC, tracer, 0)

    my_tracers = pl.ds(pl.multiple_of(plane * 128, 128), 128)

    def chemistry(i, _):
        level = jnp.where(i < 2, i + 1, 3 * (i - 2))

        @pl.when((i == 0) & jnp.logical_not(held))
        def _():
            settle(columns.at[pl.ds(1, 2), :, pl.ds(0, 248)], cell_recv.at[0])

        @pl.when(i == 2)
        def _():
            settle(columns.at[0, :, pl.ds(0, 248)], cell_recv.at[1])

        @pl.when(i == 3)
        def _():
            assemble(1)
            assemble(2)
            settle(columns.at[3, :, pl.ds(0, 248)], cell_recv.at[2])

        def cell_row(offset):
            return jnp.concatenate(
                [gathered[pl.ds((half * HALF + me) * PACK + offset + level, 1), :] for half in range(2)], axis=1
            )

        cell_sets, cell_steps = cell_row(12), cell_row(16)
        masks = [(cell_sets == k).astype(F32) for k in range(SETS)]
        by_set = source_in[...].T
        added = masks[0] * by_set[:, 0:1]
        for k in range(1, SETS):
            added = added + masks[k] * by_set[:, k : k + 1]
        masks = [m.astype(jnp.bfloat16) for m in masks]
        work[0] = jnp.concatenate([columns[level, 0], columns[level, 1]], axis=1)
        work[1] = added

        def step(turn, _):
            now = work[0]
            rounded = now.astype(jnp.bfloat16)
            chosen = jnp.concatenate([rounded * m for m in masks], axis=0)
            product = jnp.dot(matrix[...], chosen, preferred_element_type=F32)
            work[0] = jnp.where(turn.astype(F32) < cell_steps, product + work[1], now)
            return 0

        lax.fori_loop(0, NSTEP, step, 0)
        for half in range(2):
            finished[level, half] = work[0, my_tracers, pl.ds(half * LON, LON)]

        def send_back(which_plane, place):
            put(
                finished.at[level, :, pl.ds(pl.multiple_of(place * TRC, TRC), TRC)], returned.at[level, :, me],
                back_send.at[0], back_recv.at[level], device(which_plane, place),
            )

        spread(1, plane, send_back)
        returned[level, :, me] = finished[level, :, pl.ds(pl.multiple_of(me * TRC, TRC), TRC), :]
        return 0

    lax.fori_loop(0, LEV, chemistry, 0)
    assemble(0)
    assemble(3)

    settle(gathered.at[pl.ds(0, 31 * PACK)], flux_send.at[0])

    def halo_sent(side):
        settle(pack_below, halo_send.at[side, 0])
        settle(air.at[0], halo_send.at[side, 1])
        settle(raw.at[0], halo_send.at[side, 2])

    pl.when(has_below)(lambda: halo_sent(0))
    pl.when(has_above)(lambda: halo_sent(1))
    settle(columns.at[pl.ds(1, 2), :, pl.ds(0, 248)], cell_send.at[0])
    settle(columns.at[0, :, pl.ds(0, 248)], cell_send.at[1])
    settle(columns.at[3, :, pl.ds(0, 248)], cell_send.at[2])
    settle(returned.at[:, :, pl.ds(0, HALF - 1)], back_send.at[0])


def on_device(tracers, air_mass, mass_flux, chem_inverse, chem_source, reaction_set, chem_steps):
    hbm = pl.BlockSpec(memory_space=pltpu.HBM)
    dma, vmem = pltpu.SemaphoreType.DMA, pltpu.VMEM
    return pl.pallas_call(
        kernel,
        name="advect_and_react",
        out_shape=pltpu.VMEM(tracers.shape, F32),
        in_specs=[hbm] * 7,
        out_specs=pl.BlockSpec(memory_space=pltpu.VMEM),
        scratch_shapes=[
            vmem((LEV + 2,) + tracers.shape[1:], F32),
            vmem((LEV + 2, LAT, LON), F32),
            vmem(mass_flux.shape, F32),
            vmem(reaction_set.shape, jnp.int32),
            vmem(chem_steps.shape, jnp.int32),
            vmem((NT, SETS * NT), jnp.bfloat16),
            vmem((8, NT), F32),
            vmem((LAT * PACK, LON), F32),
            vmem((16, LON), F32),
            vmem((16, LON), F32),
            vmem((LEV, 6, LAT, LON), F32),
            vmem((LEV, 6, LAT, LON), F32),
            vmem((2, 6, LAT, LON), F32),
            vmem((LEV, LAT, LON), F32),
            vmem((LEV, LAT, LON), F32),
            vmem((24, LAT, LON), F32),
            vmem((12, LAT, LON), F32),
            vmem((LEV + 2, 4 * TRC + 2, LAT, LON), F32),
            vmem((HALF, 2, 2, TRC, LON), F32),
            vmem((2, HALF, 2, TRC, LON), F32),
            vmem((2, TRC, LON), F32),
            vmem((LEV, 2, NT, LON), F32),
            vmem((2, NT, 2 * LON), F32),
            vmem((LEV, 2, NT // 2, LON), F32),
            vmem((LEV, 2, HALF, TRC, LON), F32),
            dma((10,)),
            dma((1,)),
            dma((6,)),
            dma((2, 3)),
            dma((2, 3)),
            dma((3,)),
            dma((3,)),
            dma((1,)),
            dma((LEV,)),
        ],
        compiler_params=pltpu.CompilerParams(
            collective_id=0, has_side_effects=True, vmem_limit_bytes=40 * 1024 * 1024
        ),
    )(
        *(
            pltpu.with_memory_space_constraint(value, pltpu.HBM)
            for value in (
                tracers, air_mass, mass_flux, chem_inverse, chem_source, reaction_set, chem_steps
            )
        )
    )


def solution(mesh):
    return jax.shard_map(
        on_device,
        mesh=mesh,
        in_specs=(
            P("lev", "trc", None, None, None),
            P("lev", None, None),
            P(None, "lev", "trc", None),
            P(),
            P(),
            P("lev", "trc", None),
            P("lev", "trc", None),
        ),
        out_specs=P("lev", "trc", None, None, None),
        check_vma=False,
    )
```

```python
import jax
import jax.numpy as jnp
from jax import lax
from jax.experimental import pallas as pl
from jax.experimental.pallas import tpu as pltpu
from jax.sharding import PartitionSpec as P

MESH = pl.DeviceIdType.MESH
F32 = jnp.float32
LEV, TRC, LAT, LON = 4, 8, 32, 128
HALF = 16
NT, SETS, NSTEP = 256, 4, 6
PACK = 32


def lower_of(value, axis):
    return pltpu.roll(value, 1, axis)


def upper_of(value, axis):
    return pltpu.roll(value, value.shape[axis] - 1, axis)


def coefficients(air_below, air, air_above, lower, upper):
    from_below = jnp.maximum(lower, 0.0)
    from_above = jnp.maximum(-upper, 0.0)
    fraction_below = from_below / jnp.maximum(air_below, 0.5)
    fraction_above = from_above / jnp.maximum(air_above, 0.5)
    inverse = 1.0 / air
    out_up = jnp.maximum(upper, 0.0) * inverse
    out_down = jnp.maximum(-lower, 0.0) * inverse
    remain = 1.0 - out_down - out_up
    kept = air * remain
    new_air = from_below + kept + from_above
    inverse = 1.0 / new_air
    share_l, share_0, share_r = from_below * inverse, kept * inverse, from_above * inverse
    six_l, six_0, six_r = 6.0 * share_l, 6.0 * share_0, 6.0 * share_r
    return (
        new_air,
        (1.0 - fraction_below, out_down - out_up, fraction_above - 1.0, share_l, share_0, share_r),
        (
            six_l * (0.5 * share_l - 0.5),
            six_0 * (share_l + 0.5 * share_0 - 0.5),
            six_r * (0.5 - 0.5 * share_r),
            share_l * share_l * fraction_below,
            share_0 * share_0 * remain,
            share_r * share_r * fraction_above,
        ),
    )


def means(mixing, slope, first):
    (qm, q, qp), (sm, s, sp) = mixing, slope
    return qm + sm * first[0], q + s * first[1], qp + sp * first[2]


def carried(values, first):
    return first[3] * values[0] + first[4] * values[1] + first[5] * values[2]


def new_slope(mean, slope, second):
    total = second[0] * mean[0] + second[1] * mean[1] + second[2] * mean[2]
    return total + (second[3] * slope[0] + second[4] * slope[1] + second[5] * slope[2])


def around(value, axis):
    return lower_of(value, axis), value, upper_of(value, axis)


def kernel(
    tracers, air_mass, fluxes, inverse, source, sets, steps, out,
    raw, air, flux_in, sets_in, steps_in, matrix, source_in, gathered, pack_below, pack_above,
    quick_x, quick_y, quick_z, quick_air, quick_flux,
    coef, coef_z, state,
    send_mid, send_edge, send_row, columns, work, finished, returned,
    local_sem, flux_send, flux_recv, halo_send, halo_recv, cell_send, cell_recv, back_send, back_recv,
):
    t, l = lax.axis_index("trc"), lax.axis_index("lev")
    plane, me = lax.div(t, HALF), lax.rem(t, HALF)
    other = 1 - plane
    edge_row = (HALF - 1) * other
    own = pl.multiple_of(t * PACK, PACK)
    partner = other * HALF + me
    has_below, has_above = l > 0, l < 15

    def device(which_plane, place):
        return {"trc": which_plane * HALF + place, "lev": l}

    below, above = {"trc": t, "lev": l - 1}, {"trc": t, "lev": l + 1}

    def put(src, dst, send, recv, to):
        pltpu.make_async_remote_copy(
            src_ref=src, dst_ref=dst, send_sem=send, recv_sem=recv, device_id=to, device_id_type=MESH
        ).start()

    def settle(ref, sem):
        pltpu.make_async_copy(ref, ref, sem).wait()

    def spread(first_k, which_plane, start):
        def one(k, _):
            start(which_plane, lax.rem(me + k, HALF))
            return 0

        lax.fori_loop(first_k, HALF, one, 0)

    loads = [
        pltpu.make_async_copy(fluxes, flux_in, local_sem.at[0]),
        pltpu.make_async_copy(sets, sets_in, local_sem.at[1]),
        pltpu.make_async_copy(steps, steps_in, local_sem.at[2]),
        pltpu.make_async_copy(air_mass, air.at[pl.ds(1, LEV)], local_sem.at[3]),
        pltpu.make_async_copy(tracers, raw.at[pl.ds(1, LEV)], local_sem.at[4]),
        pltpu.make_async_copy(source, source_in.at[pl.ds(0, SETS)], local_sem.at[5]),
    ] + [
        pltpu.make_async_copy(inverse.at[k], matrix.at[:, pl.ds(k * NT, NT)], local_sem.at[6 + k])
        for k in range(SETS)
    ]
    for load in loads:
        load.start()

    barrier = pltpu.get_barrier_semaphore()

    def greet(to):
        pl.semaphore_signal(barrier, inc=1, device_id=to, device_id_type=MESH)

    greet(device(other, me))
    spread(1, plane, lambda which_plane, place: greet(device(which_plane, place)))
    pl.when(has_below)(lambda: greet(below))
    pl.when(has_above)(lambda: greet(above))

    for load in loads[:3]:
        load.wait()
    for level in range(LEV):
        for n in range(3):
            gathered[pl.ds(own + n * LEV + level, 1), :] = flux_in[n, level]
        gathered[pl.ds(own + 12 + level, 1), :] = sets_in[level].astype(F32)
        gathered[pl.ds(own + 16 + level, 1), :] = steps_in[level].astype(F32)
    gathered[pl.ds(own + 20, 4), :] = jnp.zeros((4, LON), F32)

    pl.semaphore_wait(barrier, HALF + has_below.astype(jnp.int32) + has_above.astype(jnp.int32))

    mine = gathered.at[pl.ds(own, 24)]
    short = gathered.at[pl.ds(own, 16)]
    put(mine, mine, flux_send.at[0], flux_recv.at[1], device(other, me))

    @pl.when(has_below)
    def _():
        put(short, pack_above.at[pl.ds(0, 16)], halo_send.at[0, 0], halo_recv.at[0, 0], below)

    @pl.when(has_above)
    def _():
        put(short, pack_below.at[pl.ds(0, 16)], halo_send.at[1, 0], halo_recv.at[1, 0], above)

    def share_own(which_plane, place):
        put(mine, mine, flux_send.at[0], flux_recv.at[0], device(which_plane, place))

    spread(1, plane, share_own)

    for load in loads[3:5]:
        load.wait()

    @pl.when(has_below)
    def _():
        put(raw.at[1], raw.at[LEV + 1], halo_send.at[0, 2], halo_recv.at[0, 2], below)
        put(air.at[1], air.at[LEV + 1], halo_send.at[0, 1], halo_recv.at[0, 1], below)

    @pl.when(has_above)
    def _():
        put(raw.at[LEV], raw.at[0], halo_send.at[1, 2], halo_recv.at[1, 2], above)
        put(air.at[LEV], air.at[0], halo_send.at[1, 1], halo_recv.at[1, 1], above)

    def wall(halo, pack):
        raw[halo] = jnp.zeros((TRC, 4, LAT, LON), F32)
        air[halo] = jnp.ones((LAT, LON), F32)
        pack[...] = jnp.zeros((24, LON), F32)

    pl.when(l == 0)(lambda: wall(0, pack_below))
    pl.when(l == 15)(lambda: wall(LEV + 1, pack_above))
    pl.when(has_below)(lambda: settle(pack_below.at[pl.ds(0, 16)], halo_recv.at[1, 0]))
    pl.when(has_above)(lambda: settle(pack_above.at[pl.ds(0, 16)], halo_recv.at[0, 0]))

    gathered[pl.ds(own + 24, 8), :] = jnp.concatenate(
        [pack_below[n * LEV + 3 : n * LEV + 4, :] for n in range(3)]
        + [pack_above[n * LEV : n * LEV + 1, :] for n in range(3)]
        + [jnp.zeros((2, LON), F32)],
        axis=0,
    )
    near = gathered.at[pl.ds(own + 24, 8)]
    put(near, near, flux_send.at[0], flux_recv.at[4], device(other, me))

    def share_near(which_plane, place):
        put(near, near, flux_send.at[0], flux_recv.at[2], device(which_plane, place))

    spread(1, plane, share_near)
    settle(gathered.at[pl.ds(0, 15 * 24)], flux_recv.at[0])

    top_level = 16 * LEV - 1
    mid_rows = send_mid.reshape((HALF + 1) * 2 * 2 * TRC, LON)
    edge_rows = send_edge.reshape(3 * HALF * 2 * TRC, LON)
    my_rows = pl.ds(pl.multiple_of(t * TRC, TRC), TRC)

    def quick(start, count, keep):
        rows, some = pl.ds(start, count), pl.ds(0, count)
        lane = lax.broadcasted_iota(jnp.int32, (count, LON), 1)
        row = lax.broadcasted_iota(jnp.int32, (count, LON), 0) + start

        def prepare(level, _):
            def flux(direction):
                return gathered[pl.ds(start * PACK + direction * LEV + level, count, stride=PACK), :]

            cell_air = air[1 + level, rows, :]
            upper = jnp.where(lane < LON - 1, flux(0), 0.0)
            new_air, first, _ = coefficients(
                lower_of(cell_air, 1), cell_air, upper_of(cell_air, 1), lower_of(upper, 1), upper
            )
            for n in range(6):
                quick_x[level, n, some] = first[n]
            upper = jnp.where(row < LAT - 1, flux(1), 0.0)
            lower = jnp.where(row > 0, lower_of(upper, 0), 0.0)
            new_air, first, _ = coefficients(
                lower_of(new_air, 0), new_air, upper_of(new_air, 0), lower, upper
            )
            for n in range(6):
                quick_y[level, n, some] = first[n]
            quick_air[level, some] = new_air
            quick_flux[level, some] = flux(2)
            return 0

        lax.fori_loop(0, LEV, prepare, 0, unroll=2 if count == HALF else 1)
        for level in (1, 2):
            _, first, _ = coefficients(
                quick_air[level - 1, some], quick_air[level, some], quick_air[level + 1, some],
                quick_flux[level - 1, some], quick_flux[level, some],
            )
            for n in range(6):
                quick_z[level - 1, n, some] = first[n]

        def tracer(n, _):
            mixing, slope = [], []
            for level in range(LEV):
                q, sx, sy, sz = (raw[1 + level, n, f, rows, :] for f in range(4))
                first = [quick_x[level, i, some] for i in range(6)]
                q = carried(means(around(q, 1), around(sx, 1), first), first)
                sy = carried(around(sy, 1), first)
                sz = carried(around(sz, 1), first)
                first = [quick_y[level, i, some] for i in range(6)]
                mixing.append(carried(means(around(q, 0), around(sy, 0), first), first))
                slope.append(carried(around(sz, 0), first))
            for level in (1, 2):
                first = [quick_z[level - 1, i, some] for i in range(6)]
                three = slice(level - 1, level + 2)
                keep(n, level - 1, carried(means(mixing[three], slope[three], first), first))
            return 0

        lax.fori_loop(0, TRC, tracer, 0, unroll=2 if count == HALF else 1)

    def keep_own_half(n, level, q):
        mid_rows[pl.ds(plane * 16 + level * TRC + n, HALF, stride=32), :] = q

    quick(pl.multiple_of(plane * HALF, HALF), HALF, keep_own_half)

    def send_own_half(which_plane, place):
        @pl.when(place != edge_row)
        def _():
            put(
                send_mid.at[place, plane], columns.at[pl.ds(1, 2), plane, my_rows],
                cell_send.at[0], cell_recv.at[0], device(which_plane, place),
            )

    spread(0, other, send_own_half)
    spread(1, plane, send_own_half)

    theirs = gathered.at[pl.ds(pl.multiple_of(partner * PACK, PACK), 24)]
    settle(theirs, flux_recv.at[1])

    def share_partner(which_plane, place):
        put(theirs, theirs, flux_send.at[0], flux_recv.at[3], device(which_plane, place))

    spread(1, plane, share_partner)
    settle(gathered.at[pl.ds(0, 15 * 24)], flux_recv.at[3])

    is_low = plane == 0

    def keep_other_half(n, level, q):
        far = jnp.where(is_low, q[HALF:], q[:HALF])
        mid_rows[pl.ds(other * 16 + level * TRC + n, HALF, stride=32), :] = far
        send_row[level, pl.ds(n, 1), :] = jnp.where(is_low, q[HALF - 1 : HALF], q[HALF : HALF + 1])

    quick(0, LAT, keep_other_half)

    def send_other_half(which_plane, place):
        put(
            send_mid.at[place, other], columns.at[pl.ds(1, 2), other, my_rows],
            cell_send.at[0], cell_recv.at[0], device(which_plane, place),
        )

        @pl.when(place == edge_row)
        def _():
            put(
                send_row.at[pl.ds(0, 2)], columns.at[pl.ds(1, 2), plane, my_rows],
                cell_send.at[0], cell_recv.at[0], device(which_plane, place),
            )

    spread(0, other, send_other_half)
    spread(1, plane, send_other_half)
    columns[pl.ds(1, 2), other, my_rows, :] = send_mid[me, other]
    columns[pl.ds(1, 2), plane, my_rows, :] = jnp.where(
        me == edge_row, send_row[pl.ds(0, 2)], send_mid[me, plane]
    )

    their_near = gathered.at[pl.ds(pl.multiple_of(partner * PACK + 24, 8), 8)]
    settle(their_near, flux_recv.at[4])

    def share_their_near(which_plane, place):
        put(their_near, their_near, flux_send.at[0], flux_recv.at[5], device(which_plane, place))

    spread(1, plane, share_their_near)

    lane = lax.broadcasted_iota(jnp.int32, (LAT, LON), 1)
    row = lax.broadcasted_iota(jnp.int32, (LAT, LON), 0)

    def horizontal(level, _):
        def flux(direction):
            inside = direction * LEV + level - 1
            place = jnp.where(level == 0, 24 + direction, jnp.where(level == LEV + 1, 27 + direction, inside))
            return gathered[pl.ds(place, LAT, stride=PACK), :]

        cell_air = air[level]
        upper = jnp.where(lane < LON - 1, flux(0), 0.0)
        new_air, first, second = coefficients(
            lower_of(cell_air, 1), cell_air, upper_of(cell_air, 1), lower_of(upper, 1), upper
        )
        for n in range(6):
            coef[n] = first[n]
            coef[6 + n] = second[n]
        upper = jnp.where(row < LAT - 1, flux(1), 0.0)
        new_air, first, second = coefficients(
            lower_of(new_air, 0), new_air, upper_of(new_air, 0), lower_of(upper, 0), upper
        )
        for n in range(6):
            coef[12 + n] = first[n]
            coef[18 + n] = second[n]
        state[level, 4 * TRC] = new_air
        state[level, 4 * TRC + 1] = jnp.where(l * LEV + level - 1 < top_level, flux(2), 0.0)

        def tracer(n, _):
            q, sx, sy, sz = (raw[level, n, f] for f in range(4))
            first = [coef[i] for i in range(6)]
            second = [coef[6 + i] for i in range(6)]
            slope = around(sx, 1)
            mean = means(around(q, 1), slope, first)
            q, sx = carried(mean, first), new_slope(mean, slope, second)
            sy, sz = carried(around(sy, 1), first), carried(around(sz, 1), first)
            first = [coef[12 + i] for i in range(6)]
            second = [coef[18 + i] for i in range(6)]
            slope = around(sy, 0)
            mean = means(around(q, 0), slope, first)
            state[level, n] = carried(mean, first)
            state[level, TRC + n] = carried(around(sz, 0), first)
            state[level, 2 * TRC + n] = carried(around(sx, 0), first)
            state[level, 3 * TRC + n] = new_slope(mean, slope, second)
            return 0

        lax.fori_loop(0, TRC, tracer, 0)
        return 0

    lax.fori_loop(1, LEV + 1, horizontal, 0)

    def vertical(level):
        at = level + 1
        _, first, second = coefficients(
            state[at - 1, 4 * TRC], state[at, 4 * TRC], state[at + 1, 4 * TRC],
            state[at - 1, 4 * TRC + 1], state[at, 4 * TRC + 1],
        )
        for i in range(6):
            coef_z[i] = first[i]
            coef_z[6 + i] = second[i]

        def tracer(n, _):
            first = [coef_z[i] for i in range(6)]
            second = [coef_z[6 + i] for i in range(6)]

            def three(f):
                return [state[at + k, f * TRC + n] for k in (-1, 0, 1)]

            slope = three(1)
            mean = means(three(0), slope, first)
            out[level, n, 0] = carried(mean, first)
            out[level, n, 3] = new_slope(mean, slope, second)
            out[level, n, 1] = carried(three(2), first)
            out[level, n, 2] = carried(three(3), first)
            return 0

        lax.fori_loop(0, TRC, tracer, 0)

    def inner_level(level, _):
        vertical(level)
        return 0

    lax.fori_loop(1, 3, inner_level, 0)

    settle(gathered.at[pl.ds(0, 15 * 8)], flux_recv.at[2])
    settle(gathered.at[pl.ds(0, 15 * 8)], flux_recv.at[5])

    @pl.when(has_below)
    def _():
        settle(air.at[0], halo_recv.at[1, 1])
        settle(raw.at[0], halo_recv.at[1, 2])

    @pl.when(has_above)
    def _():
        settle(air.at[LEV + 1], halo_recv.at[0, 1])
        settle(raw.at[LEV + 1], halo_recv.at[0, 2])

    def outer_level(i, _):
        return horizontal(i * (LEV + 1), 0)

    lax.fori_loop(0, 2, outer_level, 0)

    def edge_level(which, _):
        level = 3 * which
        vertical(level)

        def keep(n, _):
            for half in range(2):
                edge_rows[pl.ds(which * 256 + half * TRC + n, HALF, stride=16), :] = out[
                    level, n, 0, pl.ds(half * HALF, HALF), :
                ]
            return 0

        lax.fori_loop(0, TRC, keep, 0)

        def send_level(which_plane, place):
            put(
                send_edge.at[which, place], columns.at[level, :, my_rows],
                cell_send.at[1 + which], cell_recv.at[1 + which], device(which_plane, place),
            )

        spread(0, other, send_level)
        spread(1, plane, send_level)
        columns[level, :, my_rows, :] = send_edge[which, me]
        return 0

    pace = lax.div(l, 2)
    held = (pace == 5) | (pace == 6)

    @pl.when(held)
    def _():
        settle(columns.at[pl.ds(1, 2), :, pl.ds(0, 248)], cell_recv.at[0])

    lax.fori_loop(0, 2, edge_level, 0)

    for load in loads[5:]:
        load.wait()
    source_in[pl.ds(4, 4), :] = jnp.zeros((4, NT), F32)
    returned_rows = returned.reshape((LEV + 1) * 2 * HALF * TRC, LON)

    def assemble(level):
        settle(returned.at[level, :, pl.ds(0, HALF - 1)], back_recv.at[level])

        def tracer(n, _):
            for half in range(2):
                start = level * 256 + half * 128 + n
                out[level, n, 0, pl.ds(half * HALF, HALF), :] = returned_rows[
                    pl.ds(start, HALF, stride=TRC), :
                ]
            return 0

        lax.fori_loop(0, TRC, tracer, 0)

    my_tracers = pl.ds(pl.multiple_of(plane * 128, 128), 128)

    def chemistry(i, _):
        level = jnp.where(i < 2, i + 1, 3 * (i - 2))

        @pl.when((i == 0) & jnp.logical_not(held))
        def _():
            settle(columns.at[pl.ds(1, 2), :, pl.ds(0, 248)], cell_recv.at[0])

        @pl.when(i == 2)
        def _():
            settle(columns.at[0, :, pl.ds(0, 248)], cell_recv.at[1])

        @pl.when(i == 3)
        def _():
            assemble(1)
            assemble(2)
            settle(columns.at[3, :, pl.ds(0, 248)], cell_recv.at[2])

        def cell_row(offset):
            return jnp.concatenate(
                [gathered[pl.ds((half * HALF + me) * PACK + offset + level, 1), :] for half in range(2)], axis=1
            )

        cell_sets, cell_steps = cell_row(12), cell_row(16)
        masks = [(cell_sets == k).astype(F32) for k in range(SETS)]
        by_set = source_in[...].T
        added = masks[0] * by_set[:, 0:1]
        for k in range(1, SETS):
            added = added + masks[k] * by_set[:, k : k + 1]
        masks = [m.astype(jnp.bfloat16) for m in masks]
        work[0] = jnp.concatenate([columns[level, 0], columns[level, 1]], axis=1)
        work[1] = added

        def step(turn, _):
            now = work[0]
            rounded = now.astype(jnp.bfloat16)
            chosen = jnp.concatenate([rounded * m for m in masks], axis=0)
            product = jnp.dot(matrix[...], chosen, preferred_element_type=F32)
            work[0] = jnp.where(turn.astype(F32) < cell_steps, product + work[1], now)
            return 0

        lax.fori_loop(0, NSTEP, step, 0)
        for half in range(2):
            finished[level, half] = work[0, my_tracers, pl.ds(half * LON, LON)]

        def send_back(which_plane, place):
            put(
                finished.at[level, :, pl.ds(pl.multiple_of(place * TRC, TRC), TRC)], returned.at[level, :, me],
                back_send.at[0], back_recv.at[level], device(which_plane, place),
            )

        spread(1, plane, send_back)
        returned[level, :, me] = finished[level, :, pl.ds(pl.multiple_of(me * TRC, TRC), TRC), :]
        return 0

    lax.fori_loop(0, LEV, chemistry, 0)
    assemble(0)
    assemble(3)

    settle(gathered.at[pl.ds(0, 31 * PACK)], flux_send.at[0])

    def halo_sent(side):
        settle(pack_below.at[pl.ds(0, 16)], halo_send.at[side, 0])
        settle(air.at[0], halo_send.at[side, 1])
        settle(raw.at[0], halo_send.at[side, 2])

    pl.when(has_below)(lambda: halo_sent(0))
    pl.when(has_above)(lambda: halo_sent(1))
    settle(columns.at[pl.ds(1, 2), :, pl.ds(0, 248)], cell_send.at[0])
    settle(columns.at[0, :, pl.ds(0, 248)], cell_send.at[1])
    settle(columns.at[3, :, pl.ds(0, 248)], cell_send.at[2])
    settle(returned.at[pl.ds(0, LEV), :, pl.ds(0, HALF - 1)], back_send.at[0])


def on_device(tracers, air_mass, mass_flux, chem_inverse, chem_source, reaction_set, chem_steps):
    hbm = pl.BlockSpec(memory_space=pltpu.HBM)
    dma, vmem = pltpu.SemaphoreType.DMA, pltpu.VMEM
    return pl.pallas_call(
        kernel,
        name="advect_and_react",
        out_shape=pltpu.VMEM(tracers.shape, F32),
        in_specs=[hbm] * 7,
        out_specs=pl.BlockSpec(memory_space=pltpu.VMEM),
        scratch_shapes=[
            vmem((LEV + 2,) + tracers.shape[1:], F32),
            vmem((LEV + 2, LAT, LON), F32),
            vmem(mass_flux.shape, F32),
            vmem(reaction_set.shape, jnp.int32),
            vmem(chem_steps.shape, jnp.int32),
            vmem((NT, SETS * NT), jnp.bfloat16),
            vmem((8, NT), F32),
            vmem(((LAT + 1) * PACK, LON), F32),
            vmem((24, LON), F32),
            vmem((24, LON), F32),
            vmem((LEV, 6, LAT, LON), F32),
            vmem((LEV, 6, LAT, LON), F32),
            vmem((2, 6, LAT, LON), F32),
            vmem((LEV, LAT, LON), F32),
            vmem((LEV, LAT, LON), F32),
            vmem((24, LAT, LON), F32),
            vmem((12, LAT, LON), F32),
            vmem((LEV + 2, 4 * TRC + 2, LAT, LON), F32),
            vmem((HALF + 1, 2, 2, TRC, LON), F32),
            vmem((3, HALF, 2, TRC, LON), F32),
            vmem((3, TRC, LON), F32),
            vmem((LEV, 2, NT, LON), F32),
            vmem((2, NT, 2 * LON), F32),
            vmem((LEV, 2, NT // 2, LON), F32),
            vmem((LEV + 1, 2, HALF, TRC, LON), F32),
            dma((10,)),
            dma((1,)),
            dma((6,)),
            dma((2, 3)),
            dma((2, 3)),
            dma((3,)),
            dma((3,)),
            dma((1,)),
            dma((LEV,)),
        ],
        compiler_params=pltpu.CompilerParams(
            collective_id=0, has_side_effects=True, vmem_limit_bytes=40 * 1024 * 1024
        ),
    )(
        *(
            pltpu.with_memory_space_constraint(value, pltpu.HBM)
            for value in (
                tracers, air_mass, mass_flux, chem_inverse, chem_source, reaction_set, chem_steps
            )
        )
    )


def solution(mesh):
    return jax.shard_map(
        on_device,
        mesh=mesh,
        in_specs=(
            P("lev", "trc", None, None, None),
            P("lev", None, None),
            P(None, "lev", "trc", None),
            P(),
            P(),
            P("lev", "trc", None),
            P("lev", "trc", None),
        ),
        out_specs=P("lev", "trc", None, None, None),
        check_vma=False,
    )
```

```python
import jax
import jax.numpy as jnp
from jax import lax
from jax.experimental import pallas as pl
from jax.experimental.pallas import tpu as pltpu
from jax.sharding import PartitionSpec as P

MESH = pl.DeviceIdType.MESH
F32 = jnp.float32
LEV, TRC, LAT, LON = 4, 8, 32, 128
HALF = 16
NT, SETS, NSTEP = 256, 4, 6
PACK = 32


def lower_of(value, axis):
    return pltpu.roll(value, 1, axis)


def upper_of(value, axis):
    return pltpu.roll(value, value.shape[axis] - 1, axis)


def coefficients(air_below, air, air_above, lower, upper):
    from_below = jnp.maximum(lower, 0.0)
    from_above = jnp.maximum(-upper, 0.0)
    fraction_below = from_below / jnp.maximum(air_below, 0.5)
    fraction_above = from_above / jnp.maximum(air_above, 0.5)
    inverse = 1.0 / air
    out_up = jnp.maximum(upper, 0.0) * inverse
    out_down = jnp.maximum(-lower, 0.0) * inverse
    remain = 1.0 - out_down - out_up
    kept = air * remain
    new_air = from_below + kept + from_above
    inverse = 1.0 / new_air
    share_l, share_0, share_r = from_below * inverse, kept * inverse, from_above * inverse
    six_l, six_0, six_r = 6.0 * share_l, 6.0 * share_0, 6.0 * share_r
    return (
        new_air,
        (1.0 - fraction_below, out_down - out_up, fraction_above - 1.0, share_l, share_0, share_r),
        (
            six_l * (0.5 * share_l - 0.5),
            six_0 * (share_l + 0.5 * share_0 - 0.5),
            six_r * (0.5 - 0.5 * share_r),
            share_l * share_l * fraction_below,
            share_0 * share_0 * remain,
            share_r * share_r * fraction_above,
        ),
    )


def means(mixing, slope, first):
    (qm, q, qp), (sm, s, sp) = mixing, slope
    return qm + sm * first[0], q + s * first[1], qp + sp * first[2]


def carried(values, first):
    return first[3] * values[0] + first[4] * values[1] + first[5] * values[2]


def new_slope(mean, slope, second):
    total = second[0] * mean[0] + second[1] * mean[1] + second[2] * mean[2]
    return total + (second[3] * slope[0] + second[4] * slope[1] + second[5] * slope[2])


def around(value, axis):
    return lower_of(value, axis), value, upper_of(value, axis)


def kernel(
    tracers, air_mass, fluxes, inverse, source, sets, steps, out,
    raw, air, flux_in, sets_in, steps_in, matrix, source_in, gathered, pack_below, pack_above,
    quick_x, quick_y, quick_z, quick_air, quick_flux,
    coef, coef_z, state,
    send_mid, send_edge, send_row, columns, work, finished, returned,
    local_sem, flux_send, flux_recv, halo_send, halo_recv, cell_send, cell_recv, back_send, back_recv,
):
    t, l = lax.axis_index("trc"), lax.axis_index("lev")
    plane, me = lax.div(t, HALF), lax.rem(t, HALF)
    other = 1 - plane
    edge_row = (HALF - 1) * other
    own = pl.multiple_of(t * PACK, PACK)
    partner = other * HALF + me
    has_below, has_above = l > 0, l < 15

    def device(which_plane, place):
        return {"trc": which_plane * HALF + place, "lev": l}

    below, above = {"trc": t, "lev": l - 1}, {"trc": t, "lev": l + 1}

    def put(src, dst, send, recv, to):
        pltpu.make_async_remote_copy(
            src_ref=src, dst_ref=dst, send_sem=send, recv_sem=recv, device_id=to, device_id_type=MESH
        ).start()

    def settle(ref, sem):
        pltpu.make_async_copy(ref, ref, sem).wait()

    def spread(first_k, which_plane, start):
        def one(k, _):
            start(which_plane, lax.rem(me + k, HALF))
            return 0

        lax.fori_loop(first_k, HALF, one, 0)

    loads = [
        pltpu.make_async_copy(fluxes, flux_in, local_sem.at[0]),
        pltpu.make_async_copy(sets, sets_in, local_sem.at[1]),
        pltpu.make_async_copy(steps, steps_in, local_sem.at[2]),
        pltpu.make_async_copy(air_mass, air.at[pl.ds(1, LEV)], local_sem.at[3]),
        pltpu.make_async_copy(tracers, raw.at[pl.ds(1, LEV)], local_sem.at[4]),
        pltpu.make_async_copy(source, source_in.at[pl.ds(0, SETS)], local_sem.at[5]),
    ] + [
        pltpu.make_async_copy(inverse.at[k], matrix.at[:, pl.ds(k * NT, NT)], local_sem.at[6 + k])
        for k in range(SETS)
    ]
    for load in loads:
        load.start()

    barrier = pltpu.get_barrier_semaphore()

    def greet(to):
        pl.semaphore_signal(barrier, inc=1, device_id=to, device_id_type=MESH)

    greet(device(other, me))
    spread(1, plane, lambda which_plane, place: greet(device(which_plane, place)))
    pl.when(has_below)(lambda: greet(below))
    pl.when(has_above)(lambda: greet(above))

    for load in loads[:3]:
        load.wait()
    for level in range(LEV):
        for n in range(3):
            gathered[pl.ds(own + n * LEV + level, 1), :] = flux_in[n, level]
        gathered[pl.ds(own + 12 + level, 1), :] = sets_in[level].astype(F32)
        gathered[pl.ds(own + 16 + level, 1), :] = steps_in[level].astype(F32)
    gathered[pl.ds(own + 20, 4), :] = jnp.zeros((4, LON), F32)

    pl.semaphore_wait(barrier, HALF + has_below.astype(jnp.int32) + has_above.astype(jnp.int32))

    mine = gathered.at[pl.ds(own, 24)]
    short = gathered.at[pl.ds(own, 16)]
    put(mine, mine, flux_send.at[0], flux_recv.at[1], device(other, me))

    @pl.when(has_below)
    def _():
        put(short, pack_above.at[pl.ds(0, 16)], halo_send.at[0, 0], halo_recv.at[0, 0], below)

    @pl.when(has_above)
    def _():
        put(short, pack_below.at[pl.ds(0, 16)], halo_send.at[1, 0], halo_recv.at[1, 0], above)

    def share_own(which_plane, place):
        put(mine, mine, flux_send.at[0], flux_recv.at[0], device(which_plane, place))

    spread(1, plane, share_own)

    for load in loads[3:5]:
        load.wait()

    @pl.when(has_below)
    def _():
        put(raw.at[1], raw.at[LEV + 1], halo_send.at[0, 2], halo_recv.at[0, 2], below)
        put(air.at[1], air.at[LEV + 1], halo_send.at[0, 1], halo_recv.at[0, 1], below)

    @pl.when(has_above)
    def _():
        put(raw.at[LEV], raw.at[0], halo_send.at[1, 2], halo_recv.at[1, 2], above)
        put(air.at[LEV], air.at[0], halo_send.at[1, 1], halo_recv.at[1, 1], above)

    def wall(halo, pack):
        raw[halo] = jnp.zeros((TRC, 4, LAT, LON), F32)
        air[halo] = jnp.ones((LAT, LON), F32)
        pack[...] = jnp.zeros((24, LON), F32)

    pl.when(l == 0)(lambda: wall(0, pack_below))
    pl.when(l == 15)(lambda: wall(LEV + 1, pack_above))
    pl.when(has_below)(lambda: settle(pack_below.at[pl.ds(0, 16)], halo_recv.at[1, 0]))
    pl.when(has_above)(lambda: settle(pack_above.at[pl.ds(0, 16)], halo_recv.at[0, 0]))

    gathered[pl.ds(own + 24, 8), :] = jnp.concatenate(
        [pack_below[n * LEV + 3 : n * LEV + 4, :] for n in range(3)]
        + [pack_above[n * LEV : n * LEV + 1, :] for n in range(3)]
        + [jnp.zeros((2, LON), F32)],
        axis=0,
    )
    near = gathered.at[pl.ds(own + 24, 8)]
    put(near, near, flux_send.at[0], flux_recv.at[4], device(other, me))

    def share_near(which_plane, place):
        put(near, near, flux_send.at[0], flux_recv.at[2], device(which_plane, place))

    spread(1, plane, share_near)
    settle(gathered.at[pl.ds(0, 15 * 24)], flux_recv.at[0])

    top_level = 16 * LEV - 1
    mid_rows = send_mid.reshape((HALF + 1) * 2 * 2 * TRC, LON)
    edge_rows = send_edge.reshape(3 * HALF * 2 * TRC, LON)
    my_rows = pl.ds(pl.multiple_of(t * TRC, TRC), TRC)

    def quick(start, count, keep):
        rows, some = pl.ds(start, count), pl.ds(0, count)
        lane = lax.broadcasted_iota(jnp.int32, (count, LON), 1)
        row = lax.broadcasted_iota(jnp.int32, (count, LON), 0) + start

        def prepare(level, _):
            def flux(direction):
                return gathered[pl.ds(start * PACK + direction * LEV + level, count, stride=PACK), :]

            cell_air = air[1 + level, rows, :]
            upper = jnp.where(lane < LON - 1, flux(0), 0.0)
            new_air, first, _ = coefficients(
                lower_of(cell_air, 1), cell_air, upper_of(cell_air, 1), lower_of(upper, 1), upper
            )
            for n in range(6):
                quick_x[level, n, some] = first[n]
            upper = jnp.where(row < LAT - 1, flux(1), 0.0)
            lower = jnp.where(row > 0, lower_of(upper, 0), 0.0)
            new_air, first, _ = coefficients(
                lower_of(new_air, 0), new_air, upper_of(new_air, 0), lower, upper
            )
            for n in range(6):
                quick_y[level, n, some] = first[n]
            quick_air[level, some] = new_air
            quick_flux[level, some] = flux(2)
            return 0

        lax.fori_loop(0, LEV, prepare, 0, unroll=4 if count == HALF else 1)
        for level in (1, 2):
            _, first, _ = coefficients(
                quick_air[level - 1, some], quick_air[level, some], quick_air[level + 1, some],
                quick_flux[level - 1, some], quick_flux[level, some],
            )
            for n in range(6):
                quick_z[level - 1, n, some] = first[n]

        def tracer(n, _):
            mixing, slope = [], []
            for level in range(LEV):
                q, sx, sy, sz = (raw[1 + level, n, f, rows, :] for f in range(4))
                first = [quick_x[level, i, some] for i in range(6)]
                q = carried(means(around(q, 1), around(sx, 1), first), first)
                sy = carried(around(sy, 1), first)
                sz = carried(around(sz, 1), first)
                first = [quick_y[level, i, some] for i in range(6)]
                mixing.append(carried(means(around(q, 0), around(sy, 0), first), first))
                slope.append(carried(around(sz, 0), first))
            for level in (1, 2):
                first = [quick_z[level - 1, i, some] for i in range(6)]
                three = slice(level - 1, level + 2)
                keep(n, level - 1, carried(means(mixing[three], slope[three], first), first))
            return 0

        lax.fori_loop(0, TRC, tracer, 0, unroll=4 if count == HALF else 1)

    def keep_own_half(n, level, q):
        mid_rows[pl.ds(plane * 16 + level * TRC + n, HALF, stride=32), :] = q

    quick(pl.multiple_of(plane * HALF, HALF), HALF, keep_own_half)

    def send_own_half(which_plane, place):
        @pl.when(place != edge_row)
        def _():
            put(
                send_mid.at[place, plane], columns.at[pl.ds(1, 2), plane, my_rows],
                cell_send.at[0], cell_recv.at[0], device(which_plane, place),
            )

    spread(0, other, send_own_half)
    spread(1, plane, send_own_half)

    theirs = gathered.at[pl.ds(pl.multiple_of(partner * PACK, PACK), 24)]
    settle(theirs, flux_recv.at[1])

    def share_partner(which_plane, place):
        put(theirs, theirs, flux_send.at[0], flux_recv.at[3], device(which_plane, place))

    spread(1, plane, share_partner)
    settle(gathered.at[pl.ds(0, 15 * 24)], flux_recv.at[3])

    is_low = plane == 0

    def keep_other_half(n, level, q):
        far = jnp.where(is_low, q[HALF:], q[:HALF])
        mid_rows[pl.ds(other * 16 + level * TRC + n, HALF, stride=32), :] = far
        send_row[level, pl.ds(n, 1), :] = jnp.where(is_low, q[HALF - 1 : HALF], q[HALF : HALF + 1])

    quick(0, LAT, keep_other_half)

    def send_other_half(which_plane, place):
        put(
            send_mid.at[place, other], columns.at[pl.ds(1, 2), other, my_rows],
            cell_send.at[0], cell_recv.at[0], device(which_plane, place),
        )

        @pl.when(place == edge_row)
        def _():
            put(
                send_row.at[pl.ds(0, 2)], columns.at[pl.ds(1, 2), plane, my_rows],
                cell_send.at[0], cell_recv.at[0], device(which_plane, place),
            )

    spread(0, other, send_other_half)
    spread(1, plane, send_other_half)
    columns[pl.ds(1, 2), other, my_rows, :] = send_mid[me, other]
    columns[pl.ds(1, 2), plane, my_rows, :] = jnp.where(
        me == edge_row, send_row[pl.ds(0, 2)], send_mid[me, plane]
    )

    their_near = gathered.at[pl.ds(pl.multiple_of(partner * PACK + 24, 8), 8)]
    settle(their_near, flux_recv.at[4])

    def share_their_near(which_plane, place):
        put(their_near, their_near, flux_send.at[0], flux_recv.at[5], device(which_plane, place))

    spread(1, plane, share_their_near)

    lane = lax.broadcasted_iota(jnp.int32, (LAT, LON), 1)
    row = lax.broadcasted_iota(jnp.int32, (LAT, LON), 0)

    def horizontal(level, _):
        def flux(direction):
            inside = direction * LEV + level - 1
            place = jnp.where(level == 0, 24 + direction, jnp.where(level == LEV + 1, 27 + direction, inside))
            return gathered[pl.ds(place, LAT, stride=PACK), :]

        cell_air = air[level]
        upper = jnp.where(lane < LON - 1, flux(0), 0.0)
        new_air, first, second = coefficients(
            lower_of(cell_air, 1), cell_air, upper_of(cell_air, 1), lower_of(upper, 1), upper
        )
        for n in range(6):
            coef[n] = first[n]
            coef[6 + n] = second[n]
        upper = jnp.where(row < LAT - 1, flux(1), 0.0)
        new_air, first, second = coefficients(
            lower_of(new_air, 0), new_air, upper_of(new_air, 0), lower_of(upper, 0), upper
        )
        for n in range(6):
            coef[12 + n] = first[n]
            coef[18 + n] = second[n]
        state[level, 4 * TRC] = new_air
        state[level, 4 * TRC + 1] = jnp.where(l * LEV + level - 1 < top_level, flux(2), 0.0)

        def tracer(n, _):
            q, sx, sy, sz = (raw[level, n, f] for f in range(4))
            first = [coef[i] for i in range(6)]
            second = [coef[6 + i] for i in range(6)]
            slope = around(sx, 1)
            mean = means(around(q, 1), slope, first)
            q, sx = carried(mean, first), new_slope(mean, slope, second)
            sy, sz = carried(around(sy, 1), first), carried(around(sz, 1), first)
            first = [coef[12 + i] for i in range(6)]
            second = [coef[18 + i] for i in range(6)]
            slope = around(sy, 0)
            mean = means(around(q, 0), slope, first)
            state[level, n] = carried(mean, first)
            state[level, TRC + n] = carried(around(sz, 0), first)
            state[level, 2 * TRC + n] = carried(around(sx, 0), first)
            state[level, 3 * TRC + n] = new_slope(mean, slope, second)
            return 0

        lax.fori_loop(0, TRC, tracer, 0)
        return 0

    lax.fori_loop(1, LEV + 1, horizontal, 0)

    def vertical(level):
        at = level + 1
        _, first, second = coefficients(
            state[at - 1, 4 * TRC], state[at, 4 * TRC], state[at + 1, 4 * TRC],
            state[at - 1, 4 * TRC + 1], state[at, 4 * TRC + 1],
        )
        for i in range(6):
            coef_z[i] = first[i]
            coef_z[6 + i] = second[i]

        def tracer(n, _):
            first = [coef_z[i] for i in range(6)]
            second = [coef_z[6 + i] for i in range(6)]

            def three(f):
                return [state[at + k, f * TRC + n] for k in (-1, 0, 1)]

            slope = three(1)
            mean = means(three(0), slope, first)
            out[level, n, 0] = carried(mean, first)
            out[level, n, 3] = new_slope(mean, slope, second)
            out[level, n, 1] = carried(three(2), first)
            out[level, n, 2] = carried(three(3), first)
            return 0

        lax.fori_loop(0, TRC, tracer, 0)

    def inner_level(level, _):
        vertical(level)
        return 0

    lax.fori_loop(1, 3, inner_level, 0)

    settle(gathered.at[pl.ds(0, 15 * 8)], flux_recv.at[2])
    settle(gathered.at[pl.ds(0, 15 * 8)], flux_recv.at[5])

    @pl.when(has_below)
    def _():
        settle(air.at[0], halo_recv.at[1, 1])
        settle(raw.at[0], halo_recv.at[1, 2])

    @pl.when(has_above)
    def _():
        settle(air.at[LEV + 1], halo_recv.at[0, 1])
        settle(raw.at[LEV + 1], halo_recv.at[0, 2])

    def outer_level(i, _):
        return horizontal(i * (LEV + 1), 0)

    lax.fori_loop(0, 2, outer_level, 0)

    def edge_level(which, _):
        level = 3 * which
        vertical(level)

        def keep(n, _):
            for half in range(2):
                edge_rows[pl.ds(which * 256 + half * TRC + n, HALF, stride=16), :] = out[
                    level, n, 0, pl.ds(half * HALF, HALF), :
                ]
            return 0

        lax.fori_loop(0, TRC, keep, 0)

        def send_level(which_plane, place):
            put(
                send_edge.at[which, place], columns.at[level, :, my_rows],
                cell_send.at[1 + which], cell_recv.at[1 + which], device(which_plane, place),
            )

        spread(0, other, send_level)
        spread(1, plane, send_level)
        columns[level, :, my_rows, :] = send_edge[which, me]
        return 0

    pace = lax.div(l, 2)
    held = (pace == 5) | (pace == 6)

    @pl.when(held)
    def _():
        settle(columns.at[pl.ds(1, 2), :, pl.ds(0, 248)], cell_recv.at[0])

    lax.fori_loop(0, 2, edge_level, 0)

    for load in loads[5:]:
        load.wait()
    source_in[pl.ds(4, 4), :] = jnp.zeros((4, NT), F32)
    returned_rows = returned.reshape((LEV + 1) * 2 * HALF * TRC, LON)

    def assemble(level):
        settle(returned.at[level, :, pl.ds(0, HALF - 1)], back_recv.at[level])

        def tracer(n, _):
            for half in range(2):
                start = level * 256 + half * 128 + n
                out[level, n, 0, pl.ds(half * HALF, HALF), :] = returned_rows[
                    pl.ds(start, HALF, stride=TRC), :
                ]
            return 0

        lax.fori_loop(0, TRC, tracer, 0)

    my_tracers = pl.ds(pl.multiple_of(plane * 128, 128), 128)

    def chemistry(i, _):
        level = jnp.where(i < 2, i + 1, 3 * (i - 2))

        def cell_row(offset):
            return jnp.concatenate(
                [gathered[pl.ds((half * HALF + me) * PACK + offset + level, 1), :] for half in range(2)], axis=1
            )

        cell_sets, cell_steps = cell_row(12), cell_row(16)
        masks = [(cell_sets == k).astype(F32) for k in range(SETS)]
        by_set = source_in[...].T
        added = masks[0] * by_set[:, 0:1]
        for k in range(1, SETS):
            added = added + masks[k] * by_set[:, k : k + 1]
        masks = [m.astype(jnp.bfloat16) for m in masks]
        work[1] = added

        @pl.when((i == 0) & jnp.logical_not(held))
        def _():
            settle(columns.at[pl.ds(1, 2), :, pl.ds(0, 248)], cell_recv.at[0])

        @pl.when(i == 2)
        def _():
            settle(columns.at[0, :, pl.ds(0, 248)], cell_recv.at[1])

        @pl.when(i == 3)
        def _():
            assemble(1)
            assemble(2)
            settle(columns.at[3, :, pl.ds(0, 248)], cell_recv.at[2])

        work[0] = jnp.concatenate([columns[level, 0], columns[level, 1]], axis=1)

        def step(turn, _):
            now = work[0]
            rounded = now.astype(jnp.bfloat16)
            chosen = jnp.concatenate([rounded * m for m in masks], axis=0)
            product = jnp.dot(matrix[...], chosen, preferred_element_type=F32)
            work[0] = jnp.where(turn.astype(F32) < cell_steps, product + work[1], now)
            return 0

        lax.fori_loop(0, NSTEP, step, 0)
        for half in range(2):
            finished[level, half] = work[0, my_tracers, pl.ds(half * LON, LON)]

        def send_back(which_plane, place):
            put(
                finished.at[level, :, pl.ds(pl.multiple_of(place * TRC, TRC), TRC)], returned.at[level, :, me],
                back_send.at[0], back_recv.at[level], device(which_plane, place),
            )

        spread(1, plane, send_back)
        returned[level, :, me] = finished[level, :, pl.ds(pl.multiple_of(me * TRC, TRC), TRC), :]
        return 0

    lax.fori_loop(0, LEV, chemistry, 0)
    assemble(0)
    assemble(3)

    settle(gathered.at[pl.ds(0, 31 * PACK)], flux_send.at[0])

    def halo_sent(side):
        settle(pack_below.at[pl.ds(0, 16)], halo_send.at[side, 0])
        settle(air.at[0], halo_send.at[side, 1])
        settle(raw.at[0], halo_send.at[side, 2])

    pl.when(has_below)(lambda: halo_sent(0))
    pl.when(has_above)(lambda: halo_sent(1))
    settle(columns.at[pl.ds(1, 2), :, pl.ds(0, 248)], cell_send.at[0])
    settle(columns.at[0, :, pl.ds(0, 248)], cell_send.at[1])
    settle(columns.at[3, :, pl.ds(0, 248)], cell_send.at[2])
    settle(returned.at[pl.ds(0, LEV), :, pl.ds(0, HALF - 1)], back_send.at[0])


def on_device(tracers, air_mass, mass_flux, chem_inverse, chem_source, reaction_set, chem_steps):
    hbm = pl.BlockSpec(memory_space=pltpu.HBM)
    dma, vmem = pltpu.SemaphoreType.DMA, pltpu.VMEM
    return pl.pallas_call(
        kernel,
        name="advect_and_react",
        out_shape=pltpu.VMEM(tracers.shape, F32),
        in_specs=[hbm] * 7,
        out_specs=pl.BlockSpec(memory_space=pltpu.VMEM),
        scratch_shapes=[
            vmem((LEV + 2,) + tracers.shape[1:], F32),
            vmem((LEV + 2, LAT, LON), F32),
            vmem(mass_flux.shape, F32),
            vmem(reaction_set.shape, jnp.int32),
            vmem(chem_steps.shape, jnp.int32),
            vmem((NT, SETS * NT), jnp.bfloat16),
            vmem((8, NT), F32),
            vmem(((LAT + 1) * PACK, LON), F32),
            vmem((24, LON), F32),
            vmem((24, LON), F32),
            vmem((LEV, 6, LAT, LON), F32),
            vmem((LEV, 6, LAT, LON), F32),
            vmem((2, 6, LAT, LON), F32),
            vmem((LEV, LAT, LON), F32),
            vmem((LEV, LAT, LON), F32),
            vmem((24, LAT, LON), F32),
            vmem((12, LAT, LON), F32),
            vmem((LEV + 2, 4 * TRC + 2, LAT, LON), F32),
            vmem((HALF + 1, 2, 2, TRC, LON), F32),
            vmem((3, HALF, 2, TRC, LON), F32),
            vmem((3, TRC, LON), F32),
            vmem((LEV, 2, NT, LON), F32),
            vmem((2, NT, 2 * LON), F32),
            vmem((LEV, 2, NT // 2, LON), F32),
            vmem((LEV + 1, 2, HALF, TRC, LON), F32),
            dma((10,)),
            dma((1,)),
            dma((6,)),
            dma((2, 3)),
            dma((2, 3)),
            dma((3,)),
            dma((3,)),
            dma((1,)),
            dma((LEV,)),
        ],
        compiler_params=pltpu.CompilerParams(
            collective_id=0, has_side_effects=True, vmem_limit_bytes=40 * 1024 * 1024
        ),
    )(
        *(
            pltpu.with_memory_space_constraint(value, pltpu.HBM)
            for value in (
                tracers, air_mass, mass_flux, chem_inverse, chem_source, reaction_set, chem_steps
            )
        )
    )


def solution(mesh):
    return jax.shard_map(
        on_device,
        mesh=mesh,
        in_specs=(
            P("lev", "trc", None, None, None),
            P("lev", None, None),
            P(None, "lev", "trc", None),
            P(),
            P(),
            P("lev", "trc", None),
            P("lev", "trc", None),
        ),
        out_specs=P("lev", "trc", None, None, None),
        check_vma=False,
    )
```
